512 devices in a mesh: seq: 64 (over x, y, core), kv: 8 (over z).
Axes of the slice: x: 4, y: 8, z: 8, core: 2. Of those that a mesh axis runs over, the one named last changes fastest.
Arguments:
- new_hidden: bfloat16 [2, 2048, 12288], P(None, 'seq', 'kv'), may hold values from -6 to 6
- kv_weight: bfloat16 [12288, 2048], P(('kv', 'seq')), may hold values from -0.0546875 to 0.0546875
- kv_cache: bfloat16 [2, 16384, 8, 256], P(None, 'seq', 'kv'), may hold values from -4 to 4
- step_kv: bfloat16 [2, 4, 8, 256], P(None, None, 'kv'), may hold values from -12 to 12
- queries: bfloat16 [2, 4, 96, 128], P(None, None, 'kv'), may hold values from -8 to 8
- hist_len: int32 [2], replicated, may hold values from 4096 to 14336
- new_len: int32 [2], replicated, may hold values from 1 to 2048
Outputs:
- attended: bfloat16 [2, 4, 96, 128], P(None, None, 'kv')
- new_cache: bfloat16 [2, 16384, 8, 256], P(None, 'seq', 'kv')
The draws below stay inside these ranges and needn't reach their ends.
All inputs are finite; a program needn't handle non-finite values.
Results may differ from the reference program's by a relative error of at most 0.013.
Values may be sent and summed in bfloat16 or wider, within the bound.
No kernel may reach another device: no remote copies, remote signals or barrier semaphores. Data moves between devices by JAX's collectives and lax.ppermute only.
A program may use at most 64 MiB of HBM per device.

```python
import jax
import jax.numpy as jnp
from jax import lax

D = 12288
HEADS = 96
KVH = 8
HD = 128
CONV = 2
HPD = 256
STEPS = 4
QPK = 12
HIST = 16384
TURN = 2048


def draw_kv_cache(key, part):
    key = jax.random.fold_in(key, 3)
    shape = (CONV, HIST, KVH, 2 * HD)
    return jnp.clip(jax.random.normal(key, shape, jnp.float32), -4.0, 4.0).astype(jnp.bfloat16)


def draw_queries(key, part):
    key = jax.random.fold_in(key, 5)
    shape = (CONV, STEPS, HEADS, HD)
    return jnp.clip(2.5 * jax.random.normal(key, shape, jnp.float32), -8.0, 8.0).astype(jnp.bfloat16)


def ends_forced(key, lowest, highest):
    key_one, key_two, key_three = jax.random.split(key, 3)
    values = jax.random.randint(key_one, (CONV,), lowest, highest + 1)
    picked = jax.random.randint(key_two, (), 0, CONV)
    values = values.at[picked].set(highest)
    if CONV >= 3:
        other_pick = (picked + jax.random.randint(key_three, (), 1, CONV)) % CONV
        values = values.at[other_pick].set(lowest)
    return values.astype(jnp.int32)


def draw_hist_len(key, part):
    key = jax.random.fold_in(key, 7)
    return ends_forced(key, HIST // 4, HIST - TURN)


def draw_new_len(key, part):
    key = jax.random.fold_in(key, 9)
    return ends_forced(key, 1, TURN)


def block_scale(rng, dims, cuts, least, high):
    factor_of, own = 1.0, jax.random.fold_in(rng, 6)
    for dim, shards_of in cuts:
        heights = jnp.exp(jax.random.uniform(jax.random.fold_in(own, dim), (shards_of,), jnp.float32, least / len(cuts), high / len(cuts)))
        factor_of = factor_of * jnp.repeat(heights, dims[dim] // shards_of).reshape([-1 if axis == dim else 1 for axis in range(len(dims))])
    return factor_of


def gaussian(key, shape, spread, bound, cuts=(), held_as=jnp.bfloat16):
    loudness = block_scale(key, shape, cuts, -0.22, 0.18) if cuts else 1.0
    entries = jax.random.normal(key, shape, jnp.float32) * spread * loudness
    return jnp.minimum(jnp.maximum(entries, -bound), bound).astype(held_as)


def setup_inputs(seed: int = 0) -> dict:
    arg_keys = jax.random.split(jax.random.key(seed), 8)
    new_hidden = gaussian(arg_keys[0], (CONV, TURN, D), 1.0, 6.0, ((1, 64), (2, 8)))
    kv_weight = gaussian(arg_keys[1], (D, KVH * 2 * HD), D ** -0.5, 0.0546875, ((0, 512),))
    kv_cache = draw_kv_cache(jax.random.fold_in(arg_keys[7], 71), 0)
    step_kv = gaussian(arg_keys[3], (CONV, STEPS, KVH, 2 * HD), 3.0, 12.0, ((2, 8),))
    queries = draw_queries(jax.random.fold_in(arg_keys[7], 71), 0)
    hist_len = draw_hist_len(jax.random.fold_in(arg_keys[7], 71), 0)
    new_len = draw_new_len(jax.random.fold_in(arg_keys[7], 71), 0)
    return {"new_hidden": new_hidden, "kv_weight": kv_weight, "kv_cache": kv_cache, "step_kv": step_kv, "queries": queries, "hist_len": hist_len, "new_len": new_len}


rope_base = 1000000.0


def rotate(key_half, positions):
    half_size = key_half.shape[-1] // 2
    frequency = rope_base ** (-2.0 * jnp.arange(half_size, dtype=jnp.float32) / key_half.shape[-1])
    angles = positions.astype(jnp.float32)[..., None] * frequency
    cosine = jnp.cos(angles)
    sine = jnp.sin(angles)
    lower = key_half[..., :half_size]
    upper = key_half[..., half_size:]
    return jnp.concatenate([lower * cosine - upper * sine, upper * cosine + lower * sine], axis=-1)


def reference(new_hidden, kv_weight, kv_cache, step_kv, queries, hist_len, new_len):
    flat_rows = new_hidden.reshape(CONV * TURN, D)
    projected = jnp.dot(flat_rows, kv_weight, preferred_element_type=jnp.float32).reshape(CONV, TURN, KVH, 2 * HD)
    positions = hist_len[:, None] + jnp.arange(TURN, dtype=jnp.int32)[None, :]
    rotated = rotate(projected[..., :HD], positions[:, :, None])
    turn_kv = jnp.concatenate([rotated, projected[..., HD:]], axis=-1).astype(jnp.bfloat16)
    shard_count = HIST // HPD
    row_index = jnp.arange(HIST, dtype=jnp.int32)
    cache_pos = (row_index % HPD) * shard_count + row_index // HPD
    causal = jnp.arange(STEPS)[:, None] >= jnp.arange(STEPS)[None, :]
    score_scale = HD ** -0.5

    def attend_one(arguments):
        cache_rows, turn_rows, step_rows, query_rows, history, length = arguments
        offset = cache_pos - history
        written = (offset >= 0) & (offset < length)
        fetched = turn_rows[jnp.clip(offset, 0, TURN - 1).astype(jnp.int32)]
        updated = jnp.where(written[:, None, None], fetched, cache_rows)
        query_f = query_rows.astype(jnp.float32).reshape(STEPS, KVH, QPK, HD)

        def score(key_rows):
            return jnp.einsum("tgqd,rgd->tgqr", query_f, key_rows[..., :HD].astype(jnp.float32)) * score_scale

        def blend(weights, key_rows):
            return jnp.einsum("tgqr,rgd->tgqd", weights, key_rows[..., HD:].astype(jnp.float32))

        cache_score = jnp.where((cache_pos < history)[None, None, None, :], score(cache_rows), -jnp.inf)
        turn_live = jnp.arange(TURN, dtype=jnp.int32) < length
        turn_score = jnp.where(turn_live[None, None, None, :], score(turn_rows), -jnp.inf)
        step_score = jnp.where(causal[:, None, None, :], score(step_rows), -jnp.inf)
        row_max = jnp.maximum(jnp.maximum(cache_score.max(-1), turn_score.max(-1)), step_score.max(-1))
        cache_weight = jnp.exp(cache_score - row_max[..., None])
        turn_weight = jnp.exp(turn_score - row_max[..., None])
        step_weight = jnp.exp(step_score - row_max[..., None])
        totals = cache_weight.sum(-1) + turn_weight.sum(-1) + step_weight.sum(-1)
        summed = blend(cache_weight, cache_rows) + blend(turn_weight, turn_rows) + blend(step_weight, step_rows)
        attended_one = (summed / totals[..., None]).reshape(STEPS, HEADS, HD).astype(jnp.bfloat16)
        return attended_one, updated

    attended, new_cache = lax.map(attend_one, (kv_cache, turn_kv, step_kv, queries, hist_len, new_len))
    return attended, new_cache
```

```python
import jax
import jax.numpy as jnp
from jax import lax
from jax.experimental import pallas as pl
from jax.experimental.pallas import tpu as pltpu
from jax.sharding import Mesh
from jax.sharding import PartitionSpec as P

rope_base = 1000000.0
NX, NY, NC, NZ = 4, 8, 2, 8
SEQ = NX * NY * NC
GROUP = NX * NC
ALL = ("x", "y", "core", "kv")
CONV, TURN_DEV, WIDTH, HEAD, FEATURE = 2, 32, 1536, 128, 256
ROWS, SLICE = 512, 64
LOCAL = 256
STEPS, QPK = 4, 12
QROWS = STEPS * QPK
ALL_Q = CONV * QROWS
PACK = ALL_Q + 16
PIECE = 32
VMEM_LIMIT = 48 * 1024 * 1024
SMEM = pl.BlockSpec(memory_space=pltpu.SMEM)
VMEM = pl.BlockSpec(memory_space=pltpu.VMEM)


def params(flops, nbytes, limit=VMEM_LIMIT):
    return dict(
        compiler_params=pltpu.CompilerParams(vmem_limit_bytes=limit),
        cost_estimate=pl.CostEstimate(flops=flops, bytes_accessed=nbytes, transcendentals=0),
    )


def exchange(value, names):
    return lax.all_to_all(value, names, split_axis=0, concat_axis=0, tiled=True)


def lane_group(rows):
    return lax.broadcasted_iota(jnp.int32, (rows, HEAD), 1) // PIECE


def split_weight_kernel(source, out, weight):
    pltpu.sync_copy(source, weight)
    depth = weight.shape[0]
    group = lane_group(depth)
    for c in range(GROUP):
        tiles = []
        for half in range(2):
            tile = jnp.zeros((depth, HEAD), jnp.float32)
            for head in range(4 * half, 4 * half + 4):
                start = head * FEATURE + c // 4 * HEAD
                columns = weight[:, start : start + HEAD].astype(jnp.float32)
                tile = jnp.where(group == (c + head) % 4, columns, tile)
            tiles.append(tile)
        columns = jnp.concatenate(tiles, axis=1).astype(jnp.bfloat16)
        for y in range(NY):
            out[c // NC * (NY * NC) + y * NC + c % NC] = columns


def split_weight(weight):
    depth = weight.shape[0]
    return pl.pallas_call(
        split_weight_kernel,
        in_specs=[pl.BlockSpec(memory_space=pltpu.HBM)],
        scratch_shapes=[pltpu.VMEM(weight.shape, weight.dtype)],
        out_shape=jax.ShapeDtypeStruct((SEQ, depth, FEATURE), jnp.bfloat16),
        **params(1 << 20, 1 << 20, 64 * 1024 * 1024 - 128 * 1024),
    )(weight)


def project_kernel(numbers, near, near_other, far, far_other, weight, order, out):
    rows = jnp.concatenate([near[...], near_other[...], far[...], far_other[...]], axis=0)
    partial = jnp.dot(rows, weight[...], preferred_element_type=jnp.float32).astype(jnp.bfloat16)
    ordered = jnp.dot(order[...], partial, preferred_element_type=jnp.float32)
    own = numbers[6]
    group = lane_group(16)
    for owner in range(GROUP):
        for half in range(2):
            turned = []
            for part in range(4):
                start = owner * SLICE + part * 16
                tile = ordered[start : start + 16, half * HEAD : half * HEAD + HEAD]
                turned.append(pltpu.roll(tile, part * PIECE, 1) if part else tile)
            for head in range(4 * half, 4 * half + 4):
                message = turned[0]
                for part in range(1, 4):
                    message = jnp.where(group == ((own + head + part) & 3), turned[part], message)
                out[head * GROUP + owner] = message.astype(jnp.bfloat16)


def project(numbers, blocks, weight, order):
    return pl.pallas_call(
        project_kernel,
        in_specs=[SMEM] + [VMEM] * 6,
        out_specs=VMEM,
        out_shape=jax.ShapeDtypeStruct((NZ * GROUP, 16, HEAD), jnp.bfloat16),
        **params(2 * ROWS * WIDTH * FEATURE, 3 << 20),
    )(numbers, *blocks, weight, order)


def pack(average, row):
    high = row.astype(jnp.bfloat16).astype(jnp.float32)
    middle = (row - high).astype(jnp.bfloat16).astype(jnp.float32)
    low = row - high - middle
    place = lax.broadcasted_iota(jnp.int32, (16, HEAD), 0)
    stats = jnp.where(place == 0, high, jnp.where(place == 1, middle, jnp.where(place == 2, low, 0.0)))
    return jnp.concatenate([average, stats], axis=0).astype(jnp.bfloat16)


def diagonal(first):
    row = lax.broadcasted_iota(jnp.int32, (ALL_Q, HEAD), 0)
    return row + first == lax.broadcasted_iota(jnp.int32, (ALL_Q, HEAD), 1)


def merge(parts, first):
    rows = []
    for part in parts:
        stats = part[first + ALL_Q : first + PACK].astype(jnp.float32)
        rows.append(stats[0:1] + stats[1:2] + stats[2:3])
    lses = jnp.concatenate(rows, axis=0)
    top = jnp.max(lses, axis=0, keepdims=True)
    weights = jnp.exp(lses - top)
    total = jnp.sum(weights, axis=0, keepdims=True)
    weights = weights / total
    on_diagonal = diagonal(first)
    summed = jnp.zeros((ALL_Q, HEAD), jnp.float32)
    for index, part in enumerate(parts):
        spread = jnp.where(on_diagonal, weights[index : index + 1], 0.0).astype(jnp.bfloat16)
        summed += jnp.dot(spread, part, preferred_element_type=jnp.float32)
    return summed, top + jnp.log(total)


def history_kernel(numbers, cache, step_kv, queries, summed, tops, totals):
    t = numbers[4]
    for conv in range(CONV):
        history, length = numbers[conv], numbers[2 + conv]
        query = queries[conv]
        keys = [cache[conv, :, :HEAD], step_kv[conv, :, :HEAD]]
        values = [cache[conv, :, HEAD:], step_kv[conv, :, HEAD:]]
        position = lax.broadcasted_iota(jnp.int32, (QROWS, LOCAL), 1) * SEQ + t
        step = lax.broadcasted_iota(jnp.int32, (QROWS, 16), 1)
        asked = lax.broadcasted_iota(jnp.int32, (QROWS, 16), 0) & 3
        visible = [
            position < history,
            (step <= asked) & (((history + length + step) & (SEQ - 1)) == t),
        ]
        scores = [score(query, rows) for rows in keys]
        top = jnp.maximum(*[largest(one, seen) for one, seen in zip(scores, visible)])
        weights = [jnp.where(seen, jnp.exp(one - top), 0.0) for one, seen in zip(scores, visible)]
        total = sum(jnp.sum(weight, axis=1, keepdims=True) for weight in weights)
        rows = slice(conv * QROWS, conv * QROWS + QROWS)
        summed[rows] = sum(blend(weight, value) for weight, value in zip(weights, values))
        tops[rows] = jnp.broadcast_to(top, (QROWS, HEAD))
        totals[rows] = jnp.broadcast_to(total, (QROWS, HEAD))


def score(query, rows):
    contract = (((1,), (1,)), ((), ()))
    return lax.dot_general(query, rows, contract, preferred_element_type=jnp.float32) * HEAD ** (-0.5)


def largest(scores, seen):
    return jnp.max(jnp.where(seen, scores, -3e38), axis=1, keepdims=True)


def blend(weights, rows):
    return jnp.dot(weights.astype(jnp.bfloat16), rows, preferred_element_type=jnp.float32)


def attend_history(numbers, cache, step_kv, queries):
    return pl.pallas_call(
        history_kernel,
        in_specs=[SMEM] + [VMEM] * 3,
        out_specs=[VMEM] * 3,
        out_shape=[jax.ShapeDtypeStruct((ALL_Q, HEAD), jnp.float32)] * 3,
        **params(2 * ALL_Q * LOCAL * FEATURE, 1 << 20),
    )(numbers, cache, step_kv, queries)


def attend_kernel(numbers, arrived, cosine, sine, queries, summed, tops, totals, out):
    y, own, z = numbers[5], numbers[6], numbers[7]
    group = lane_group(16)
    sums = []
    for c in range(GROUP):
        total = arrived[c].astype(jnp.float32)
        for plane in range(1, NZ):
            total += arrived[plane * GROUP + c].astype(jnp.float32)
        sums.append(total)
    halves = []
    for tile in range(2):
        pieces = []
        for part in range(4):
            piece = sums[4 * tile]
            for c in range(4 * tile + 1, 4 * tile + 4):
                piece = jnp.where(group == ((c + z + part) & 3), sums[c], piece)
            pieces.append(pltpu.roll(piece, HEAD - part * PIECE, 1) if part else piece)
        halves.append(jnp.concatenate(pieces, axis=0))
    key, value = halves
    key = key * cosine[...] + pltpu.roll(key, HEAD // 2, 1) * sine[...]
    for row in range(NY):
        both = jnp.concatenate([key[row * 8 : row * 8 + 8], value[row * 8 : row * 8 + 8]], axis=0)
        out[row, :16] = both.astype(jnp.bfloat16)
    key, value = key.astype(jnp.bfloat16), value.astype(jnp.bfloat16)

    asker = lax.broadcasted_iota(jnp.int32, (ALL_Q, SLICE), 0) >= QROWS
    row = lax.broadcasted_iota(jnp.int32, (ALL_Q, SLICE), 1)
    history = jnp.where(asker, numbers[1], numbers[0])
    length = jnp.where(asker, numbers[3], numbers[2])
    owner = own // NC * (NY * NC) + (row >> 3) * NC + own % NC
    offset = ((row & 3) * NY + y) * SEQ + ((owner - history) & (SEQ - 1))
    visible = (((row >> 2) & 1) == asker.astype(jnp.int32)) & (offset < length)
    scores = score(jnp.concatenate([queries[0], queries[1]], axis=0), key)
    old_top = tops[:, :1]
    top = jnp.maximum(old_top, largest(scores, visible))
    weights = jnp.where(visible, jnp.exp(scores - top), 0.0)
    kept = jnp.exp(old_top - top)
    total = totals[:, :1] * kept + jnp.sum(weights, axis=1, keepdims=True)
    average = (summed[...] * kept + blend(weights, value)) / total
    lse = jnp.sum(jnp.where(diagonal(16), top + jnp.log(total), 0.0), axis=0, keepdims=True)
    packed = pack(average, lse)
    for row in range(NY):
        out[row, 16:] = packed


def attend(numbers, arrived, cosine, sine, queries, history):
    return pl.pallas_call(
        attend_kernel,
        in_specs=[SMEM] + [VMEM] * 7,
        out_specs=VMEM,
        out_shape=jax.ShapeDtypeStruct((NY, 16 + PACK, HEAD), jnp.bfloat16),
        **params(4 * ALL_Q * SLICE * HEAD, 1 << 20),
    )(numbers, arrived, cosine, sine, queries, *history)


def merge_kernel(arrived, out):
    average, lse = merge([arrived[row] for row in range(NY)], 16)
    lse = pltpu.roll(jnp.broadcast_to(lse, (8, HEAD)), HEAD - 16, 1)[0:1]
    packed = pack(average, lse)
    for device in range(GROUP):
        out[device] = packed


def finish_kernel(arrived, out):
    rest = jnp.zeros((HEAD - PACK, HEAD), jnp.bfloat16)
    parts = [jnp.concatenate([arrived[device], rest], axis=0) for device in range(GROUP)]
    out[...] = merge(parts, 0)[0].astype(jnp.bfloat16)


def combine(kernel, shape, arrived):
    return pl.pallas_call(
        kernel,
        out_shape=jax.ShapeDtypeStruct(shape, jnp.bfloat16),
        **params(PACK * HEAD * 32, 1 << 19),
    )(arrived)


def write_kernel(numbers, arrived, cache, new_cache):
    t = numbers[4]
    rows = jnp.concatenate([arrived[row, :16].astype(jnp.float32) for row in range(NY)], axis=0)
    rows = rows.astype(jnp.bfloat16)
    for conv in range(CONV):
        history, length = numbers[conv], numbers[2 + conv]
        within = (t - history) & (SEQ - 1)
        first = lax.div(history + within, SEQ)
        row = lax.broadcasted_iota(jnp.int32, (LOCAL, HEAD), 0) - first
        column = lax.broadcasted_iota(jnp.int32, (LOCAL, HEAD), 1)
        slot = (column & 3) * NY + (column >> 4)
        live = (((column >> 2) & 1) == conv) & (slot * SEQ + within < length) & (row == slot)
        written = (row >= 0) & (row < 32) & (row * SEQ + within < length)
        for half in range(2):
            place = jnp.where(live & (((column >> 3) & 1) == half), 1.0, 0.0).astype(jnp.bfloat16)
            placed = jnp.dot(place, rows, preferred_element_type=jnp.float32)
            lanes = slice(half * HEAD, half * HEAD + HEAD)
            kept = jnp.where(written, placed, cache[conv, :, lanes].astype(jnp.float32))
            new_cache[conv, :, lanes] = kept.astype(jnp.bfloat16)


def write(numbers, arrived, cache):
    return pl.pallas_call(
        write_kernel,
        in_specs=[SMEM] + [VMEM] * 2,
        out_specs=VMEM,
        out_shape=jax.ShapeDtypeStruct((CONV, LOCAL, FEATURE), jnp.bfloat16),
        **params(4 * CONV * LOCAL * HEAD * FEATURE, 1 << 20),
    )(numbers, arrived, cache)


def on_device(new_hidden, kv_weight, kv_cache, step_kv, queries, hist_len, new_len):
    x, y, core, z = (lax.axis_index(name) for name in ALL)
    t = (x * NY + y) * NC + core
    own = x * NC + core

    weight = exchange(split_weight(kv_weight), ("x", "y", "core")).reshape(WIDTH, FEATURE)

    swap = [(0, 1), (1, 0)]
    there, back = [], []
    for chip in range(NX):
        for side, step in ((0, NX - 1), (1, 1)):
            there.append((chip * NC + side, (chip + step) % NX * NC + side))
            back.append((chip * NC + side, (chip - step) % NX * NC + side))
    hidden = new_hidden.reshape(CONV * TURN_DEV, WIDTH)
    after = lax.ppermute(hidden, ("x", "core"), there)
    hidden, after = lax.optimization_barrier((hidden, after))
    before = lax.ppermute(hidden, ("x", "core"), back)
    near = jnp.concatenate([hidden, after], axis=0)
    far = jnp.concatenate([before, lax.ppermute(after, ("x", "core"), there)], axis=0)
    near_other = lax.ppermute(near, "core", swap)
    near_other, hist_len, new_len = lax.optimization_barrier((near_other, hist_len, new_len))
    blocks = [near, near_other, far, lax.ppermute(far, "core", swap)]
    numbers = jnp.concatenate([hist_len, new_len, jnp.stack([t, y, own, z])]).astype(jnp.int32)

    def axis(size, place):
        shape = [1, 1, 1, 1]
        shape[place] = size
        return jnp.arange(size, dtype=jnp.int32).reshape(shape)

    history = hist_len.reshape(1, 1, CONV, 1)
    source_x = axis(NX, 3)

    def within_of(device):
        owner = device // NC * (NY * NC) + axis(NY, 1) * NC + device % NC
        return (owner - history) % SEQ

    within = within_of(axis(GROUP, 0))
    crossed = within // TURN_DEV ^ core
    place = jnp.where(within // TURN_DEV == 0, source_x - x, x - source_x) % NX
    place = jnp.where(place < 2, place, 7 - place) + crossed * 2
    column = place * SLICE + axis(CONV, 2) * TURN_DEV + within % TURN_DEV
    order = (column.reshape(ROWS, 1) == jnp.arange(ROWS, dtype=jnp.int32)[None, :]).astype(jnp.bfloat16)

    position = history + (source_x * NY + y) * SEQ + within_of(own)
    frequency = rope_base ** (-2.0 * jnp.arange(HEAD // 2, dtype=jnp.float32) / HEAD)
    angles = position.reshape(SLICE, 1).astype(jnp.float32) * frequency[None, :]
    cosine, sine = jnp.cos(angles), jnp.sin(angles)
    cosine = jnp.concatenate([cosine, cosine], axis=1)
    sine = jnp.concatenate([-sine, sine], axis=1)

    asked = queries.transpose(0, 2, 1, 3).reshape(CONV, QROWS, HEAD)
    steps = jnp.pad(step_kv.reshape(CONV, STEPS, FEATURE), ((0, 0), (0, 16 - STEPS), (0, 0)))
    cache = kv_cache.reshape(CONV, LOCAL, FEATURE)

    partial = exchange(project(numbers, blocks, weight, order), ("kv", "x", "core"))
    history_part = attend_history(numbers, cache, steps, asked)
    rows = exchange(attend(numbers, partial, cosine, sine, asked, history_part), ("y",))
    packed = exchange(combine(merge_kernel, (GROUP, PACK, HEAD), rows), ("x", "core"))
    new_cache = write(numbers, rows, cache)
    attended = combine(finish_kernel, (ALL_Q, HEAD), packed)
    attended = attended.reshape(CONV, QPK, STEPS, HEAD).transpose(0, 2, 1, 3)
    return attended, new_cache.reshape(kv_cache.shape)


def solution(mesh):
    split = Mesh(mesh.devices.reshape(NX, NY, NC, NZ), ALL)
    seq = ALL[:3]
    return jax.shard_map(
        on_device,
        mesh=split,
        in_specs=(
            P(None, seq, "kv"),
            P(("kv",) + seq, None),
            P(None, seq, "kv", None),
            P(None, None, "kv", None),
            P(None, None, "kv", None),
            P(),
            P(),
        ),
        out_specs=(P(None, None, "kv", None), P(None, seq, "kv", None)),
        check_vma=False,
    )
```

```python
import jax
import jax.numpy as jnp
from jax import lax
from jax.experimental import pallas as pl
from jax.experimental.pallas import tpu as pltpu
from jax.sharding import Mesh
from jax.sharding import PartitionSpec as P

rope_base = 1000000.0
NX, NY, NC, NZ = 4, 8, 2, 8
SEQ = NX * NY * NC
GROUP = NX * NC
ALL = ("x", "y", "core", "kv")
CONV, TURN_DEV, WIDTH, HEAD, FEATURE = 2, 32, 1536, 128, 256
ROWS, SLICE = 512, 64
LOCAL = 256
STEPS, QPK = 4, 12
QROWS = STEPS * QPK
ALL_Q = CONV * QROWS
PACK = ALL_Q + 16
PIECE = 32
FIRST = 6 * GROUP + 2 * NC
VMEM_LIMIT = 48 * 1024 * 1024
SMEM = pl.BlockSpec(memory_space=pltpu.SMEM)
VMEM = pl.BlockSpec(memory_space=pltpu.VMEM)


def params(flops, nbytes):
    return dict(
        compiler_params=pltpu.CompilerParams(vmem_limit_bytes=VMEM_LIMIT),
        cost_estimate=pl.CostEstimate(flops=flops, bytes_accessed=nbytes, transcendentals=0),
    )


def exchange(value, names, order=None):
    groups = None if order is None else [order]
    return lax.all_to_all(value, names, split_axis=0, concat_axis=0, tiled=True, axis_index_groups=groups)


def lane_group(rows):
    return lax.broadcasted_iota(jnp.int32, (rows, HEAD), 1) // PIECE


def split_weight_kernel(source, out, weight):
    pltpu.sync_copy(source, weight)
    depth = weight.shape[0]
    group = lane_group(depth)
    for c in range(GROUP):
        tiles = []
        for half in range(2):
            tile = jnp.zeros((depth, HEAD), jnp.float32)
            for head in range(4 * half, 4 * half + 4):
                start = head * FEATURE + c // 4 * HEAD
                columns = weight[:, start : start + HEAD].astype(jnp.float32)
                tile = jnp.where(group == (c + head) % 4, columns, tile)
            tiles.append(tile)
        columns = jnp.concatenate(tiles, axis=1).astype(jnp.bfloat16)
        for y in range(NY):
            out[c // NC * (NY * NC) + y * NC + c % NC] = columns


def split_weight(weight):
    depth = weight.shape[0]
    return pl.pallas_call(
        split_weight_kernel,
        in_specs=[pl.BlockSpec(memory_space=pltpu.HBM)],
        scratch_shapes=[pltpu.VMEM(weight.shape, weight.dtype)],
        out_shape=jax.ShapeDtypeStruct((SEQ, depth, FEATURE), jnp.bfloat16),
        **params(1 << 20, 1 << 20),
    )(weight)


def project_kernel(numbers, near, near_other, far, far_other, weight, order, out):
    rows = jnp.concatenate([near[...], near_other[...], far[...], far_other[...]], axis=0)
    partial = jnp.dot(rows, weight[...], preferred_element_type=jnp.float32).astype(jnp.bfloat16)
    ordered = jnp.dot(order[...], partial, preferred_element_type=jnp.float32)
    own = numbers[6]
    group = lane_group(16)
    for owner in range(GROUP):
        for half in range(2):
            turned = []
            for part in range(4):
                start = owner * SLICE + part * 16
                tile = ordered[start : start + 16, half * HEAD : half * HEAD + HEAD]
                turned.append(pltpu.roll(tile, part * PIECE, 1) if part else tile)
            for head in range(4 * half, 4 * half + 4):
                message = turned[0]
                for part in range(1, 4):
                    message = jnp.where(group == ((own + head + part) & 3), turned[part], message)
                out[(head * GROUP + owner - FIRST) % (NZ * GROUP)] = message.astype(jnp.bfloat16)


def project(numbers, blocks, weight, order):
    return pl.pallas_call(
        project_kernel,
        in_specs=[SMEM] + [VMEM] * 6,
        out_specs=VMEM,
        out_shape=jax.ShapeDtypeStruct((NZ * GROUP, 16, HEAD), jnp.bfloat16),
        **params(2 * ROWS * WIDTH * FEATURE, 3 << 20),
    )(numbers, *blocks, weight, order)


def pack(average, row):
    high = row.astype(jnp.bfloat16).astype(jnp.float32)
    middle = (row - high).astype(jnp.bfloat16).astype(jnp.float32)
    low = row - high - middle
    place = lax.broadcasted_iota(jnp.int32, (16, HEAD), 0)
    stats = jnp.where(place == 0, high, jnp.where(place == 1, middle, jnp.where(place == 2, low, 0.0)))
    return jnp.concatenate([average, stats], axis=0).astype(jnp.bfloat16)


def diagonal(first):
    row = lax.broadcasted_iota(jnp.int32, (ALL_Q, HEAD), 0)
    return row + first == lax.broadcasted_iota(jnp.int32, (ALL_Q, HEAD), 1)


def merge(parts, first):
    rows = []
    for part in parts:
        stats = part[first + ALL_Q : first + PACK].astype(jnp.float32)
        rows.append(stats[0:1] + stats[1:2] + stats[2:3])
    lses = jnp.concatenate(rows, axis=0)
    top = jnp.max(lses, axis=0, keepdims=True)
    weights = jnp.exp(lses - top)
    total = jnp.sum(weights, axis=0, keepdims=True)
    weights = weights / total
    on_diagonal = diagonal(first)
    summed = jnp.zeros((ALL_Q, HEAD), jnp.float32)
    spread = [
        jnp.where(on_diagonal, weights[index : index + 1], 0.0).astype(jnp.bfloat16)
        for index in range(len(parts))
    ]
    for index in range(0, len(parts), 2):
        pair = jnp.concatenate(spread[index : index + 2], axis=1)
        both = jnp.concatenate(parts[index : index + 2], axis=0)
        summed += jnp.dot(pair, both, preferred_element_type=jnp.float32)
    return summed, top + jnp.log(total)


def history_kernel(numbers, cache, step_kv, queries, summed, tops, totals):
    t = numbers[4]
    for conv in range(CONV):
        history, length = numbers[conv], numbers[2 + conv]
        query = queries[conv]
        keys = [cache[conv, :, :HEAD], step_kv[conv, :, :HEAD]]
        values = [cache[conv, :, HEAD:], step_kv[conv, :, HEAD:]]
        position = lax.broadcasted_iota(jnp.int32, (QROWS, LOCAL), 1) * SEQ + t
        step = lax.broadcasted_iota(jnp.int32, (QROWS, 16), 1)
        asked = lax.broadcasted_iota(jnp.int32, (QROWS, 16), 0) & 3
        visible = [
            position < history,
            (step <= asked) & (((history + length + step) & (SEQ - 1)) == t),
        ]
        scores = [score(query, rows) for rows in keys]
        top = jnp.maximum(*[largest(one, seen) for one, seen in zip(scores, visible)])
        weights = [jnp.where(seen, jnp.exp(one - top), 0.0) for one, seen in zip(scores, visible)]
        total = sum(jnp.sum(weight, axis=1, keepdims=True) for weight in weights)
        rows = slice(conv * QROWS, conv * QROWS + QROWS)
        summed[rows] = sum(blend(weight, value) for weight, value in zip(weights, values))
        tops[rows] = jnp.broadcast_to(top, (QROWS, HEAD))
        totals[rows] = jnp.broadcast_to(total, (QROWS, HEAD))


def score(query, rows):
    contract = (((1,), (1,)), ((), ()))
    return lax.dot_general(query, rows, contract, preferred_element_type=jnp.float32) * HEAD ** (-0.5)


def largest(scores, seen):
    return jnp.max(jnp.where(seen, scores, -3e38), axis=1, keepdims=True)


def blend(weights, rows):
    return jnp.dot(weights.astype(jnp.bfloat16), rows, preferred_element_type=jnp.float32)


def attend_history(numbers, cache, step_kv, queries):
    return pl.pallas_call(
        history_kernel,
        in_specs=[SMEM] + [VMEM] * 3,
        out_specs=[VMEM] * 3,
        out_shape=[jax.ShapeDtypeStruct((ALL_Q, HEAD), jnp.float32)] * 3,
        **params(2 * ALL_Q * LOCAL * FEATURE, 1 << 20),
    )(numbers, cache, step_kv, queries)


def attend_kernel(numbers, arrived, cosine, sine, queries, summed, tops, totals, out):
    y, own, z = numbers[5], numbers[6], numbers[7]
    group = lane_group(16)
    sums = []
    for c in range(GROUP):
        total = arrived[(c - FIRST) % (NZ * GROUP)].astype(jnp.float32)
        for plane in range(1, NZ):
            total += arrived[(plane * GROUP + c - FIRST) % (NZ * GROUP)].astype(jnp.float32)
        sums.append(total)
    halves = []
    for tile in range(2):
        pieces = []
        for part in range(4):
            piece = sums[4 * tile]
            for c in range(4 * tile + 1, 4 * tile + 4):
                piece = jnp.where(group == ((c + z + part) & 3), sums[c], piece)
            pieces.append(pltpu.roll(piece, HEAD - part * PIECE, 1) if part else piece)
        halves.append(jnp.concatenate(pieces, axis=0))
    key, value = halves
    key = key * cosine[...] + pltpu.roll(key, HEAD // 2, 1) * sine[...]
    for row in range(NY):
        both = jnp.concatenate([key[row * 8 : row * 8 + 8], value[row * 8 : row * 8 + 8]], axis=0)
        out[row, :16] = both.astype(jnp.bfloat16)
    key, value = key.astype(jnp.bfloat16), value.astype(jnp.bfloat16)

    asker = lax.broadcasted_iota(jnp.int32, (ALL_Q, SLICE), 0) >= QROWS
    row = lax.broadcasted_iota(jnp.int32, (ALL_Q, SLICE), 1)
    history = jnp.where(asker, numbers[1], numbers[0])
    length = jnp.where(asker, numbers[3], numbers[2])
    owner = own // NC * (NY * NC) + (row >> 3) * NC + own % NC
    offset = ((row & 3) * NY + y) * SEQ + ((owner - history) & (SEQ - 1))
    visible = (((row >> 2) & 1) == asker.astype(jnp.int32)) & (offset < length)
    scores = score(jnp.concatenate([queries[0], queries[1]], axis=0), key)
    old_top = tops[:, :1]
    top = jnp.maximum(old_top, largest(scores, visible))
    weights = jnp.where(visible, jnp.exp(scores - top), 0.0)
    kept = jnp.exp(old_top - top)
    total = totals[:, :1] * kept + jnp.sum(weights, axis=1, keepdims=True)
    average = (summed[...] * kept + blend(weights, value)) / total
    lse = jnp.sum(jnp.where(diagonal(16), top + jnp.log(total), 0.0), axis=0, keepdims=True)
    packed = pack(average, lse)
    for row in range(NY):
        out[row, 16:] = packed


def attend(numbers, arrived, cosine, sine, queries, history):
    return pl.pallas_call(
        attend_kernel,
        in_specs=[SMEM] + [VMEM] * 7,
        out_specs=VMEM,
        out_shape=jax.ShapeDtypeStruct((NY, 16 + PACK, HEAD), jnp.bfloat16),
        **params(4 * ALL_Q * SLICE * HEAD, 1 << 20),
    )(numbers, arrived, cosine, sine, queries, *history)


def merge_kernel(arrived, out):
    average, lse = merge([arrived[row] for row in range(NY)], 16)
    lse = pltpu.roll(jnp.broadcast_to(lse, (8, HEAD)), HEAD - 16, 1)[0:1]
    packed = pack(average, lse)
    for device in range(GROUP):
        out[device] = packed


def finish_kernel(arrived, out):
    rest = jnp.zeros((HEAD - PACK, HEAD), jnp.bfloat16)
    parts = [jnp.concatenate([arrived[device], rest], axis=0) for device in range(GROUP)]
    out[...] = merge(parts, 0)[0].astype(jnp.bfloat16)


def combine(kernel, shape, arrived):
    return pl.pallas_call(
        kernel,
        out_shape=jax.ShapeDtypeStruct(shape, jnp.bfloat16),
        **params(PACK * HEAD * 32, 1 << 19),
    )(arrived)


def write_kernel(numbers, arrived, cache, new_cache):
    t = numbers[4]
    rows = jnp.concatenate([arrived[row, :16].astype(jnp.float32) for row in range(NY)], axis=0)
    rows = rows.astype(jnp.bfloat16)
    for conv in range(CONV):
        history, length = numbers[conv], numbers[2 + conv]
        within = (t - history) & (SEQ - 1)
        first = lax.div(history + within, SEQ)
        row = lax.broadcasted_iota(jnp.int32, (LOCAL, HEAD), 0) - first
        column = lax.broadcasted_iota(jnp.int32, (LOCAL, HEAD), 1)
        slot = (column & 3) * NY + (column >> 4)
        live = (((column >> 2) & 1) == conv) & (slot * SEQ + within < length) & (row == slot)
        written = (row >= 0) & (row < 32) & (row * SEQ + within < length)
        for half in range(2):
            place = jnp.where(live & (((column >> 3) & 1) == half), 1.0, 0.0).astype(jnp.bfloat16)
            placed = jnp.dot(place, rows, preferred_element_type=jnp.float32)
            lanes = slice(half * HEAD, half * HEAD + HEAD)
            kept = jnp.where(written, placed, cache[conv, :, lanes].astype(jnp.float32))
            new_cache[conv, :, lanes] = kept.astype(jnp.bfloat16)


def write(numbers, arrived, cache):
    return pl.pallas_call(
        write_kernel,
        in_specs=[SMEM] + [VMEM] * 2,
        out_specs=VMEM,
        out_shape=jax.ShapeDtypeStruct((CONV, LOCAL, FEATURE), jnp.bfloat16),
        **params(4 * CONV * LOCAL * HEAD * FEATURE, 1 << 20),
    )(numbers, arrived, cache)


def on_device(new_hidden, kv_weight, kv_cache, step_kv, queries, hist_len, new_len):
    x, y, core, z = (lax.axis_index(name) for name in ALL)
    t = (x * NY + y) * NC + core
    own = x * NC + core

    weight = exchange(split_weight(kv_weight), ("x", "y", "core")).reshape(WIDTH, FEATURE)

    swap = [(0, 1), (1, 0)]
    there, back = [], []
    for chip in range(NX):
        for side, step in ((0, NX - 1), (1, 1)):
            there.append((chip * NC + side, (chip + step) % NX * NC + side))
            back.append((chip * NC + side, (chip - step) % NX * NC + side))
    hidden = new_hidden.reshape(CONV * TURN_DEV, WIDTH)
    after = lax.ppermute(hidden, ("x", "core"), there)
    hidden, after = lax.optimization_barrier((hidden, after))
    before = lax.ppermute(hidden, ("x", "core"), back)
    near = jnp.concatenate([hidden, after], axis=0)
    far = jnp.concatenate([before, lax.ppermute(after, ("x", "core"), there)], axis=0)
    near_other = lax.ppermute(near, "core", swap)
    near_other, hist_len, new_len = lax.optimization_barrier((near_other, hist_len, new_len))
    blocks = [near, near_other, far, lax.ppermute(far, "core", swap)]
    numbers = jnp.concatenate([hist_len, new_len, jnp.stack([t, y, own, z])]).astype(jnp.int32)

    def axis(size, place):
        shape = [1, 1, 1, 1]
        shape[place] = size
        return jnp.arange(size, dtype=jnp.int32).reshape(shape)

    history = hist_len.reshape(1, 1, CONV, 1)
    source_x = axis(NX, 3)

    def within_of(device):
        owner = device // NC * (NY * NC) + axis(NY, 1) * NC + device % NC
        return (owner - history) % SEQ

    within = within_of(axis(GROUP, 0))
    crossed = within // TURN_DEV ^ core
    place = jnp.where(within // TURN_DEV == 0, source_x - x, x - source_x) % NX
    place = jnp.where(place < 2, place, 7 - place) + crossed * 2
    column = place * SLICE + axis(CONV, 2) * TURN_DEV + within % TURN_DEV
    order = (column.reshape(ROWS, 1) == jnp.arange(ROWS, dtype=jnp.int32)[None, :]).astype(jnp.bfloat16)

    position = history + (source_x * NY + y) * SEQ + within_of(own)
    frequency = rope_base ** (-2.0 * jnp.arange(HEAD // 2, dtype=jnp.float32) / HEAD)
    angles = position.reshape(SLICE, 1).astype(jnp.float32) * frequency[None, :]
    cosine, sine = jnp.cos(angles), jnp.sin(angles)
    cosine = jnp.concatenate([cosine, cosine], axis=1)
    sine = jnp.concatenate([-sine, sine], axis=1)

    asked = queries.transpose(0, 2, 1, 3).reshape(CONV, QROWS, HEAD)
    steps = jnp.pad(step_kv.reshape(CONV, STEPS, FEATURE), ((0, 0), (0, 16 - STEPS), (0, 0)))
    cache = kv_cache.reshape(CONV, LOCAL, FEATURE)

    members = [(place + FIRST) % (NZ * GROUP) for place in range(NZ * GROUP)]
    partial = exchange(project(numbers, blocks, weight, order), ("kv", "x", "core"), members)
    history_part = attend_history(numbers, cache, steps, asked)
    rows = exchange(attend(numbers, partial, cosine, sine, asked, history_part), ("y",))
    packed = exchange(combine(merge_kernel, (GROUP, PACK, HEAD), rows), ("x", "core"))
    new_cache = write(numbers, rows, cache)
    attended = combine(finish_kernel, (ALL_Q, HEAD), packed)
    attended = attended.reshape(CONV, QPK, STEPS, HEAD).transpose(0, 2, 1, 3)
    return attended, new_cache.reshape(kv_cache.shape)


def solution(mesh):
    split = Mesh(mesh.devices.reshape(NX, NY, NC, NZ), ALL)
    seq = ALL[:3]
    return jax.shard_map(
        on_device,
        mesh=split,
        in_specs=(
            P(None, seq, "kv"),
            P(("kv",) + seq, None),
            P(None, seq, "kv", None),
            P(None, None, "kv", None),
            P(None, None, "kv", None),
            P(),
            P(),
        ),
        out_specs=(P(None, None, "kv", None), P(None, seq, "kv", None)),
        check_vma=False,
    )
```

```python
import jax
import jax.numpy as jnp
from jax import lax
from jax.experimental import pallas as pl
from jax.experimental.pallas import tpu as pltpu
from jax.sharding import Mesh
from jax.sharding import PartitionSpec as P

rope_base = 1000000.0
NX, NY, NC, NZ = 4, 8, 2, 8
SEQ = NX * NY * NC
GROUP = NX * NC
ALL = ("x", "y", "core", "kv")
CONV, TURN_DEV, WIDTH, HEAD, FEATURE = 2, 32, 1536, 128, 256
ROWS, SLICE = 512, 64
LOCAL = 256
STEPS, QPK = 4, 12
QROWS = STEPS * QPK
ALL_Q = CONV * QROWS
PACK = ALL_Q + 16
PIECE = 32
FIRST_SEQ = (2 * NY + 6) * NC
FIRST = 6 * GROUP + 2 * NC
FIRST_Y = 4
VMEM_LIMIT = 48 * 1024 * 1024
SMEM = pl.BlockSpec(memory_space=pltpu.SMEM)
VMEM = pl.BlockSpec(memory_space=pltpu.VMEM)


def params(flops, nbytes):
    return dict(
        compiler_params=pltpu.CompilerParams(vmem_limit_bytes=VMEM_LIMIT),
        cost_estimate=pl.CostEstimate(flops=flops, bytes_accessed=nbytes, transcendentals=0),
    )


def exchange(value, names, first=0):
    size = value.shape[0]
    groups = [[(place + first) % size for place in range(size)]] if first else None
    return lax.all_to_all(value, names, split_axis=0, concat_axis=0, tiled=True, axis_index_groups=groups)


def lane_group(rows):
    return lax.broadcasted_iota(jnp.int32, (rows, HEAD), 1) // PIECE


def split_weight_kernel(source, out, weight):
    pltpu.sync_copy(source, weight)
    depth = weight.shape[0]
    group = lane_group(depth)
    for c in range(GROUP):
        tiles = []
        for half in range(2):
            tile = jnp.zeros((depth, HEAD), jnp.float32)
            for head in range(4 * half, 4 * half + 4):
                start = head * FEATURE + c // 4 * HEAD
                columns = weight[:, start : start + HEAD].astype(jnp.float32)
                tile = jnp.where(group == (c + head) % 4, columns, tile)
            tiles.append(tile)
        columns = jnp.concatenate(tiles, axis=1).astype(jnp.bfloat16)
        for y in range(NY):
            out[(c // NC * (NY * NC) + y * NC + c % NC - FIRST_SEQ) % SEQ] = columns


def split_weight(weight):
    depth = weight.shape[0]
    return pl.pallas_call(
        split_weight_kernel,
        in_specs=[pl.BlockSpec(memory_space=pltpu.HBM)],
        scratch_shapes=[pltpu.VMEM(weight.shape, weight.dtype)],
        out_shape=jax.ShapeDtypeStruct((SEQ, depth, FEATURE), jnp.bfloat16),
        **params(1 << 20, 1 << 20),
    )(weight)


def project_kernel(numbers, near, near_other, far, far_other, weight, order, out):
    rows = jnp.concatenate([near[...], near_other[...], far[...], far_other[...]], axis=0)
    start = (SEQ - FIRST_SEQ) * (WIDTH // SEQ)
    weights = jnp.concatenate([weight[start:], weight[:start]], axis=0)
    partial = jnp.dot(rows, weights, preferred_element_type=jnp.float32).astype(jnp.bfloat16)
    ordered = jnp.dot(order[...], partial, preferred_element_type=jnp.float32)
    own = numbers[6]
    group = lane_group(16)
    for owner in range(GROUP):
        for half in range(2):
            turned = []
            for part in range(4):
                start = owner * SLICE + part * 16
                tile = ordered[start : start + 16, half * HEAD : half * HEAD + HEAD]
                turned.append(pltpu.roll(tile, part * PIECE, 1) if part else tile)
            for head in range(4 * half, 4 * half + 4):
                message = turned[0]
                for part in range(1, 4):
                    message = jnp.where(group == ((own + head + part) & 3), turned[part], message)
                out[(head * GROUP + owner - FIRST) % (NZ * GROUP)] = message.astype(jnp.bfloat16)


def project(numbers, blocks, weight, order):
    return pl.pallas_call(
        project_kernel,
        in_specs=[SMEM] + [VMEM] * 6,
        out_specs=VMEM,
        out_shape=jax.ShapeDtypeStruct((NZ * GROUP, 16, HEAD), jnp.bfloat16),
        **params(2 * ROWS * WIDTH * FEATURE, 3 << 20),
    )(numbers, *blocks, weight, order)


def pack(average, row):
    high = row.astype(jnp.bfloat16).astype(jnp.float32)
    middle = (row - high).astype(jnp.bfloat16).astype(jnp.float32)
    low = row - high - middle
    place = lax.broadcasted_iota(jnp.int32, (16, HEAD), 0)
    stats = jnp.where(place == 0, high, jnp.where(place == 1, middle, jnp.where(place == 2, low, 0.0)))
    return jnp.concatenate([average, stats], axis=0).astype(jnp.bfloat16)


def diagonal(first):
    row = lax.broadcasted_iota(jnp.int32, (ALL_Q, HEAD), 0)
    return row + first == lax.broadcasted_iota(jnp.int32, (ALL_Q, HEAD), 1)


def merge(parts, first):
    rows = []
    for part in parts:
        stats = part[first + ALL_Q : first + PACK].astype(jnp.float32)
        rows.append(stats[0:1] + stats[1:2] + stats[2:3])
    lses = jnp.concatenate(rows, axis=0)
    top = jnp.max(lses, axis=0, keepdims=True)
    weights = jnp.exp(lses - top)
    total = jnp.sum(weights, axis=0, keepdims=True)
    weights = weights / total
    on_diagonal = diagonal(first)
    summed = jnp.zeros((ALL_Q, HEAD), jnp.float32)
    spread = [
        jnp.where(on_diagonal, weights[index : index + 1], 0.0).astype(jnp.bfloat16)
        for index in range(len(parts))
    ]
    for index in range(0, len(parts), 2):
        pair = jnp.concatenate(spread[index : index + 2], axis=1)
        both = jnp.concatenate(parts[index : index + 2], axis=0)
        summed += jnp.dot(pair, both, preferred_element_type=jnp.float32)
    return summed, top + jnp.log(total)


def history_kernel(numbers, cache, step_kv, queries, summed, tops, totals):
    t = numbers[4]
    for conv in range(CONV):
        history, length = numbers[conv], numbers[2 + conv]
        query = queries[conv]
        keys = [cache[conv, :, :HEAD], step_kv[conv, :, :HEAD]]
        values = [cache[conv, :, HEAD:], step_kv[conv, :, HEAD:]]
        position = lax.broadcasted_iota(jnp.int32, (QROWS, LOCAL), 1) * SEQ + t
        step = lax.broadcasted_iota(jnp.int32, (QROWS, 16), 1)
        asked = lax.broadcasted_iota(jnp.int32, (QROWS, 16), 0) & 3
        visible = [
            position < history,
            (step <= asked) & (((history + length + step) & (SEQ - 1)) == t),
        ]
        scores = [score(query, rows) for rows in keys]
        top = jnp.maximum(*[largest(one, seen) for one, seen in zip(scores, visible)])
        weights = [jnp.where(seen, jnp.exp(one - top), 0.0) for one, seen in zip(scores, visible)]
        total = sum(jnp.sum(weight, axis=1, keepdims=True) for weight in weights)
        rows = slice(conv * QROWS, conv * QROWS + QROWS)
        summed[rows] = sum(blend(weight, value) for weight, value in zip(weights, values))
        tops[rows] = jnp.broadcast_to(top, (QROWS, HEAD))
        totals[rows] = jnp.broadcast_to(total, (QROWS, HEAD))


def score(query, rows):
    contract = (((1,), (1,)), ((), ()))
    return lax.dot_general(query, rows, contract, preferred_element_type=jnp.float32) * HEAD ** (-0.5)


def largest(scores, seen):
    return jnp.max(jnp.where(seen, scores, -3e38), axis=1, keepdims=True)


def blend(weights, rows):
    return jnp.dot(weights.astype(jnp.bfloat16), rows, preferred_element_type=jnp.float32)


def attend_history(numbers, cache, step_kv, queries):
    return pl.pallas_call(
        history_kernel,
        in_specs=[SMEM] + [VMEM] * 3,
        out_specs=[VMEM] * 3,
        out_shape=[jax.ShapeDtypeStruct((ALL_Q, HEAD), jnp.float32)] * 3,
        **params(2 * ALL_Q * LOCAL * FEATURE, 1 << 20),
    )(numbers, cache, step_kv, queries)


def attend_kernel(numbers, arrived, cosine, sine, queries, summed, tops, totals, out):
    y, own, z = numbers[5], numbers[6], numbers[7]
    group = lane_group(16)
    sums = []
    for c in range(GROUP):
        total = arrived[(c - FIRST) % (NZ * GROUP)].astype(jnp.float32)
        for plane in range(1, NZ):
            total += arrived[(plane * GROUP + c - FIRST) % (NZ * GROUP)].astype(jnp.float32)
        sums.append(total)
    halves = []
    for tile in range(2):
        pieces = []
        for part in range(4):
            piece = sums[4 * tile]
            for c in range(4 * tile + 1, 4 * tile + 4):
                piece = jnp.where(group == ((c + z + part) & 3), sums[c], piece)
            pieces.append(pltpu.roll(piece, HEAD - part * PIECE, 1) if part else piece)
        halves.append(jnp.concatenate(pieces, axis=0))
    key, value = halves
    key = key * cosine[...] + pltpu.roll(key, HEAD // 2, 1) * sine[...]
    for row in range(NY):
        both = jnp.concatenate([key[row * 8 : row * 8 + 8], value[row * 8 : row * 8 + 8]], axis=0)
        out[(row - FIRST_Y) % NY, :16] = both.astype(jnp.bfloat16)
    key, value = key.astype(jnp.bfloat16), value.astype(jnp.bfloat16)

    asker = lax.broadcasted_iota(jnp.int32, (ALL_Q, SLICE), 0) >= QROWS
    row = lax.broadcasted_iota(jnp.int32, (ALL_Q, SLICE), 1)
    history = jnp.where(asker, numbers[1], numbers[0])
    length = jnp.where(asker, numbers[3], numbers[2])
    owner = own // NC * (NY * NC) + (row >> 3) * NC + own % NC
    offset = ((row & 3) * NY + y) * SEQ + ((owner - history) & (SEQ - 1))
    visible = (((row >> 2) & 1) == asker.astype(jnp.int32)) & (offset < length)
    scores = score(jnp.concatenate([queries[0], queries[1]], axis=0), key)
    old_top = tops[:, :1]
    top = jnp.maximum(old_top, largest(scores, visible))
    weights = jnp.where(visible, jnp.exp(scores - top), 0.0)
    kept = jnp.exp(old_top - top)
    total = totals[:, :1] * kept + jnp.sum(weights, axis=1, keepdims=True)
    average = (summed[...] * kept + blend(weights, value)) / total
    lse = jnp.sum(jnp.where(diagonal(16), top + jnp.log(total), 0.0), axis=0, keepdims=True)
    packed = pack(average, lse)
    for row in range(NY):
        out[row, 16:] = packed


def attend(numbers, arrived, cosine, sine, queries, history):
    return pl.pallas_call(
        attend_kernel,
        in_specs=[SMEM] + [VMEM] * 7,
        out_specs=VMEM,
        out_shape=jax.ShapeDtypeStruct((NY, 16 + PACK, HEAD), jnp.bfloat16),
        **params(4 * ALL_Q * SLICE * HEAD, 1 << 20),
    )(numbers, arrived, cosine, sine, queries, *history)


def merge_kernel(arrived, out):
    average, lse = merge([arrived[row] for row in range(NY)], 16)
    lse = pltpu.roll(jnp.broadcast_to(lse, (8, HEAD)), HEAD - 16, 1)[0:1]
    packed = pack(average, lse)
    for device in range(GROUP):
        out[device] = packed


def finish_kernel(arrived, out):
    rest = jnp.zeros((HEAD - PACK, HEAD), jnp.bfloat16)
    parts = [jnp.concatenate([arrived[device], rest], axis=0) for device in range(GROUP)]
    out[...] = merge(parts, 0)[0].astype(jnp.bfloat16)


def combine(kernel, shape, arrived):
    return pl.pallas_call(
        kernel,
        out_shape=jax.ShapeDtypeStruct(shape, jnp.bfloat16),
        **params(PACK * HEAD * 32, 1 << 19),
    )(arrived)


def write_kernel(numbers, arrived, cache, new_cache):
    t = numbers[4]
    rows = jnp.concatenate([arrived[(row - FIRST_Y) % NY, :16].astype(jnp.float32) for row in range(NY)], axis=0)
    rows = rows.astype(jnp.bfloat16)
    for conv in range(CONV):
        history, length = numbers[conv], numbers[2 + conv]
        within = (t - history) & (SEQ - 1)
        first = lax.div(history + within, SEQ)
        row = lax.broadcasted_iota(jnp.int32, (LOCAL, HEAD), 0) - first
        column = lax.broadcasted_iota(jnp.int32, (LOCAL, HEAD), 1)
        slot = (column & 3) * NY + (column >> 4)
        live = (((column >> 2) & 1) == conv) & (slot * SEQ + within < length) & (row == slot)
        written = (row >= 0) & (row < 32) & (row * SEQ + within < length)
        for half in range(2):
            place = jnp.where(live & (((column >> 3) & 1) == half), 1.0, 0.0).astype(jnp.bfloat16)
            placed = jnp.dot(place, rows, preferred_element_type=jnp.float32)
            lanes = slice(half * HEAD, half * HEAD + HEAD)
            kept = jnp.where(written, placed, cache[conv, :, lanes].astype(jnp.float32))
            new_cache[conv, :, lanes] = kept.astype(jnp.bfloat16)


def write(numbers, arrived, cache):
    return pl.pallas_call(
        write_kernel,
        in_specs=[SMEM] + [VMEM] * 2,
        out_specs=VMEM,
        out_shape=jax.ShapeDtypeStruct((CONV, LOCAL, FEATURE), jnp.bfloat16),
        **params(4 * CONV * LOCAL * HEAD * FEATURE, 1 << 20),
    )(numbers, arrived, cache)


def on_device(new_hidden, kv_weight, kv_cache, step_kv, queries, hist_len, new_len):
    x, y, core, z = (lax.axis_index(name) for name in ALL)
    t = (x * NY + y) * NC + core
    own = x * NC + core

    weight = exchange(split_weight(kv_weight), ("x", "y", "core"), FIRST_SEQ).reshape(WIDTH, FEATURE)

    swap = [(0, 1), (1, 0)]
    there, back = [], []
    for chip in range(NX):
        for side, step in ((0, NX - 1), (1, 1)):
            there.append((chip * NC + side, (chip + step) % NX * NC + side))
            back.append((chip * NC + side, (chip - step) % NX * NC + side))
    hidden = new_hidden.reshape(CONV * TURN_DEV, WIDTH)
    after = lax.ppermute(hidden, ("x", "core"), there)
    hidden, after = lax.optimization_barrier((hidden, after))
    before = lax.ppermute(hidden, ("x", "core"), back)
    near = jnp.concatenate([hidden, after], axis=0)
    far = jnp.concatenate([before, lax.ppermute(after, ("x", "core"), there)], axis=0)
    near_other = lax.ppermute(near, "core", swap)
    near_other, hist_len, new_len = lax.optimization_barrier((near_other, hist_len, new_len))
    blocks = [near, near_other, far, lax.ppermute(far, "core", swap)]
    numbers = jnp.concatenate([hist_len, new_len, jnp.stack([t, y, own, z])]).astype(jnp.int32)

    def axis(size, place):
        shape = [1, 1, 1, 1]
        shape[place] = size
        return jnp.arange(size, dtype=jnp.int32).reshape(shape)

    history = hist_len.reshape(1, 1, CONV, 1)
    source_x = axis(NX, 3)

    def within_of(device):
        owner = device // NC * (NY * NC) + axis(NY, 1) * NC + device % NC
        return (owner - history) % SEQ

    within = within_of(axis(GROUP, 0))
    crossed = within // TURN_DEV ^ core
    place = jnp.where(within // TURN_DEV == 0, source_x - x, x - source_x) % NX
    place = jnp.where(place < 2, place, 7 - place) + crossed * 2
    column = place * SLICE + axis(CONV, 2) * TURN_DEV + within % TURN_DEV
    order = (column.reshape(ROWS, 1) == jnp.arange(ROWS, dtype=jnp.int32)[None, :]).astype(jnp.bfloat16)

    position = history + (source_x * NY + y) * SEQ + within_of(own)
    frequency = rope_base ** (-2.0 * jnp.arange(HEAD // 2, dtype=jnp.float32) / HEAD)
    angles = position.reshape(SLICE, 1).astype(jnp.float32) * frequency[None, :]
    cosine, sine = jnp.cos(angles), jnp.sin(angles)
    cosine = jnp.concatenate([cosine, cosine], axis=1)
    sine = jnp.concatenate([-sine, sine], axis=1)

    asked = queries.transpose(0, 2, 1, 3).reshape(CONV, QROWS, HEAD)
    steps = jnp.pad(step_kv.reshape(CONV, STEPS, FEATURE), ((0, 0), (0, 16 - STEPS), (0, 0)))
    cache = kv_cache.reshape(CONV, LOCAL, FEATURE)

    partial = exchange(project(numbers, blocks, weight, order), ("kv", "x", "core"), FIRST)
    history_part = attend_history(numbers, cache, steps, asked)
    rows = exchange(attend(numbers, partial, cosine, sine, asked, history_part), ("y",), FIRST_Y)
    packed = exchange(combine(merge_kernel, (GROUP, PACK, HEAD), rows), ("x", "core"))
    new_cache = write(numbers, rows, cache)
    attended = combine(finish_kernel, (ALL_Q, HEAD), packed)
    attended = attended.reshape(CONV, QPK, STEPS, HEAD).transpose(0, 2, 1, 3)
    return attended, new_cache.reshape(kv_cache.shape)


def solution(mesh):
    split = Mesh(mesh.devices.reshape(NX, NY, NC, NZ), ALL)
    seq = ALL[:3]
    return jax.shard_map(
        on_device,
        mesh=split,
        in_specs=(
            P(None, seq, "kv"),
            P(("kv",) + seq, None),
            P(None, seq, "kv", None),
            P(None, None, "kv", None),
            P(None, None, "kv", None),
            P(),
            P(),
        ),
        out_specs=(P(None, None, "kv", None), P(None, seq, "kv", None)),
        check_vma=False,
    )
```

```python
import jax
import jax.numpy as jnp
from jax import lax
from jax.experimental import pallas as pl
from jax.experimental.pallas import tpu as pltpu
from jax.sharding import Mesh
from jax.sharding import PartitionSpec as P

rope_base = 1000000.0
NX, NY, NC, NZ = 4, 8, 2, 8
SEQ = NX * NY * NC
GROUP = NX * NC
ALL = ("x", "y", "core", "kv")
CONV, TURN_DEV, WIDTH, HEAD, FEATURE = 2, 32, 1536, 128, 256
ROWS, SLICE = 512, 64
LOCAL = 256
STEPS, QPK = 4, 12
QROWS = STEPS * QPK
ALL_Q = CONV * QROWS
PACK = ALL_Q + 16
PIECE = 32
FIRST_SEQ = (2 * NY + 6) * NC
FIRST = 6 * GROUP + 2 * NC
FIRST_Y = 4
FIRST_GROUP = 2 * NC
VMEM_LIMIT = 48 * 1024 * 1024
SMEM = pl.BlockSpec(memory_space=pltpu.SMEM)
VMEM = pl.BlockSpec(memory_space=pltpu.VMEM)


def params(flops, nbytes):
    return dict(
        compiler_params=pltpu.CompilerParams(vmem_limit_bytes=VMEM_LIMIT),
        cost_estimate=pl.CostEstimate(flops=flops, bytes_accessed=nbytes, transcendentals=0),
    )


def exchange(value, names, first=0):
    size = value.shape[0]
    groups = [[(place + first) % size for place in range(size)]] if first else None
    return lax.all_to_all(value, names, split_axis=0, concat_axis=0, tiled=True, axis_index_groups=groups)


def lane_group(rows):
    return lax.broadcasted_iota(jnp.int32, (rows, HEAD), 1) // PIECE


def split_weight_kernel(source, out, weight):
    pltpu.sync_copy(source, weight)
    depth = weight.shape[0]
    group = lane_group(depth)
    for c in range(GROUP):
        tiles = []
        for half in range(2):
            tile = jnp.zeros((depth, HEAD), jnp.float32)
            for head in range(4 * half, 4 * half + 4):
                start = head * FEATURE + c // 4 * HEAD
                columns = weight[:, start : start + HEAD].astype(jnp.float32)
                tile = jnp.where(group == (c + head) % 4, columns, tile)
            tiles.append(tile)
        columns = jnp.concatenate(tiles, axis=1).astype(jnp.bfloat16)
        for y in range(NY):
            out[(c // NC * (NY * NC) + y * NC + c % NC - FIRST_SEQ) % SEQ] = columns


def split_weight(weight):
    depth = weight.shape[0]
    return pl.pallas_call(
        split_weight_kernel,
        in_specs=[pl.BlockSpec(memory_space=pltpu.HBM)],
        scratch_shapes=[pltpu.VMEM(weight.shape, weight.dtype)],
        out_shape=jax.ShapeDtypeStruct((SEQ, depth, FEATURE), jnp.bfloat16),
        **params(1 << 20, 1 << 20),
    )(weight)


def project_kernel(numbers, near, near_other, far, far_other, weight, order, out):
    rows = jnp.concatenate([near[...], near_other[...], far[...], far_other[...]], axis=0)
    start = (SEQ - FIRST_SEQ) * (WIDTH // SEQ)
    weights = jnp.concatenate([weight[start:], weight[:start]], axis=0)
    partial = jnp.dot(rows, weights, preferred_element_type=jnp.float32).astype(jnp.bfloat16)
    ordered = jnp.dot(order[...], partial, preferred_element_type=jnp.float32)
    own = numbers[6]
    group = lane_group(16)
    for owner in range(GROUP):
        for half in range(2):
            turned = []
            for part in range(4):
                start = owner * SLICE + part * 16
                tile = ordered[start : start + 16, half * HEAD : half * HEAD + HEAD]
                turned.append(pltpu.roll(tile, part * PIECE, 1) if part else tile)
            for head in range(4 * half, 4 * half + 4):
                message = turned[0]
                for part in range(1, 4):
                    message = jnp.where(group == ((own + head + part) & 3), turned[part], message)
                out[(head * GROUP + owner - FIRST) % (NZ * GROUP)] = message.astype(jnp.bfloat16)


def project(numbers, blocks, weight, order):
    return pl.pallas_call(
        project_kernel,
        in_specs=[SMEM] + [VMEM] * 6,
        out_specs=VMEM,
        out_shape=jax.ShapeDtypeStruct((NZ * GROUP, 16, HEAD), jnp.bfloat16),
        **params(2 * ROWS * WIDTH * FEATURE, 3 << 20),
    )(numbers, *blocks, weight, order)


def pack(average, row):
    high = row.astype(jnp.bfloat16).astype(jnp.float32)
    middle = (row - high).astype(jnp.bfloat16).astype(jnp.float32)
    low = row - high - middle
    place = lax.broadcasted_iota(jnp.int32, (16, HEAD), 0)
    stats = jnp.where(place == 0, high, jnp.where(place == 1, middle, jnp.where(place == 2, low, 0.0)))
    return jnp.concatenate([average, stats], axis=0).astype(jnp.bfloat16)


def diagonal(first):
    row = lax.broadcasted_iota(jnp.int32, (ALL_Q, HEAD), 0)
    return row + first == lax.broadcasted_iota(jnp.int32, (ALL_Q, HEAD), 1)


def merge(parts, first):
    rows = []
    for part in parts:
        stats = part[first + ALL_Q : first + PACK].astype(jnp.float32)
        rows.append(stats[0:1] + stats[1:2] + stats[2:3])
    lses = jnp.concatenate(rows, axis=0)
    top = jnp.max(lses, axis=0, keepdims=True)
    weights = jnp.exp(lses - top)
    total = jnp.sum(weights, axis=0, keepdims=True)
    weights = weights / total
    on_diagonal = diagonal(first)
    summed = jnp.zeros((ALL_Q, HEAD), jnp.float32)
    spread = [
        jnp.where(on_diagonal, weights[index : index + 1], 0.0).astype(jnp.bfloat16)
        for index in range(len(parts))
    ]
    for index in range(0, len(parts), 2):
        pair = jnp.concatenate(spread[index : index + 2], axis=1)
        both = jnp.concatenate(parts[index : index + 2], axis=0)
        summed += jnp.dot(pair, both, preferred_element_type=jnp.float32)
    return summed, top + jnp.log(total)


def history_kernel(numbers, cache, step_kv, queries, summed, tops, totals):
    t = numbers[4]
    for conv in range(CONV):
        history, length = numbers[conv], numbers[2 + conv]
        query = queries[conv]
        keys = [cache[conv, :, :HEAD], step_kv[conv, :, :HEAD]]
        values = [cache[conv, :, HEAD:], step_kv[conv, :, HEAD:]]
        position = lax.broadcasted_iota(jnp.int32, (QROWS, LOCAL), 1) * SEQ + t
        step = lax.broadcasted_iota(jnp.int32, (QROWS, 16), 1)
        asked = lax.broadcasted_iota(jnp.int32, (QROWS, 16), 0) & 3
        visible = [
            position < history,
            (step <= asked) & (((history + length + step) & (SEQ - 1)) == t),
        ]
        scores = [score(query, rows) for rows in keys]
        top = jnp.maximum(*[largest(one, seen) for one, seen in zip(scores, visible)])
        weights = [jnp.where(seen, jnp.exp(one - top), 0.0) for one, seen in zip(scores, visible)]
        total = sum(jnp.sum(weight, axis=1, keepdims=True) for weight in weights)
        rows = slice(conv * QROWS, conv * QROWS + QROWS)
        summed[rows] = sum(blend(weight, value) for weight, value in zip(weights, values))
        tops[rows] = jnp.broadcast_to(top, (QROWS, HEAD))
        totals[rows] = jnp.broadcast_to(total, (QROWS, HEAD))


def score(query, rows):
    contract = (((1,), (1,)), ((), ()))
    return lax.dot_general(query, rows, contract, preferred_element_type=jnp.float32) * HEAD ** (-0.5)


def largest(scores, seen):
    return jnp.max(jnp.where(seen, scores, -3e38), axis=1, keepdims=True)


def blend(weights, rows):
    return jnp.dot(weights.astype(jnp.bfloat16), rows, preferred_element_type=jnp.float32)


def attend_history(numbers, cache, step_kv, queries):
    return pl.pallas_call(
        history_kernel,
        in_specs=[SMEM] + [VMEM] * 3,
        out_specs=[VMEM] * 3,
        out_shape=[jax.ShapeDtypeStruct((ALL_Q, HEAD), jnp.float32)] * 3,
        **params(2 * ALL_Q * LOCAL * FEATURE, 1 << 20),
    )(numbers, cache, step_kv, queries)


def attend_kernel(numbers, arrived, cosine, sine, queries, summed, tops, totals, out):
    y, own, z = numbers[5], numbers[6], numbers[7]
    group = lane_group(16)
    sums = []
    for c in range(GROUP):
        total = arrived[(c - FIRST) % (NZ * GROUP)].astype(jnp.float32)
        for plane in range(1, NZ):
            total += arrived[(plane * GROUP + c - FIRST) % (NZ * GROUP)].astype(jnp.float32)
        sums.append(total)
    halves = []
    for tile in range(2):
        pieces = []
        for part in range(4):
            piece = sums[4 * tile]
            for c in range(4 * tile + 1, 4 * tile + 4):
                piece = jnp.where(group == ((c + z + part) & 3), sums[c], piece)
            pieces.append(pltpu.roll(piece, HEAD - part * PIECE, 1) if part else piece)
        halves.append(jnp.concatenate(pieces, axis=0))
    key, value = halves
    key = key * cosine[...] + pltpu.roll(key, HEAD // 2, 1) * sine[...]
    for row in range(NY):
        both = jnp.concatenate([key[row * 8 : row * 8 + 8], value[row * 8 : row * 8 + 8]], axis=0)
        out[(row - FIRST_Y) % NY, :16] = both.astype(jnp.bfloat16)
    key, value = key.astype(jnp.bfloat16), value.astype(jnp.bfloat16)

    asker = lax.broadcasted_iota(jnp.int32, (ALL_Q, SLICE), 0) >= QROWS
    row = lax.broadcasted_iota(jnp.int32, (ALL_Q, SLICE), 1)
    history = jnp.where(asker, numbers[1], numbers[0])
    length = jnp.where(asker, numbers[3], numbers[2])
    owner = own // NC * (NY * NC) + (row >> 3) * NC + own % NC
    offset = ((row & 3) * NY + y) * SEQ + ((owner - history) & (SEQ - 1))
    visible = (((row >> 2) & 1) == asker.astype(jnp.int32)) & (offset < length)
    scores = score(jnp.concatenate([queries[0], queries[1]], axis=0), key)
    old_top = tops[:, :1]
    top = jnp.maximum(old_top, largest(scores, visible))
    weights = jnp.where(visible, jnp.exp(scores - top), 0.0)
    kept = jnp.exp(old_top - top)
    total = totals[:, :1] * kept + jnp.sum(weights, axis=1, keepdims=True)
    average = (summed[...] * kept + blend(weights, value)) / total
    lse = jnp.sum(jnp.where(diagonal(16), top + jnp.log(total), 0.0), axis=0, keepdims=True)
    packed = pack(average, lse)
    for row in range(NY):
        out[row, 16:] = packed


def attend(numbers, arrived, cosine, sine, queries, history):
    return pl.pallas_call(
        attend_kernel,
        in_specs=[SMEM] + [VMEM] * 7,
        out_specs=VMEM,
        out_shape=jax.ShapeDtypeStruct((NY, 16 + PACK, HEAD), jnp.bfloat16),
        **params(4 * ALL_Q * SLICE * HEAD, 1 << 20),
    )(numbers, arrived, cosine, sine, queries, *history)


def merge_kernel(arrived, out):
    average, lse = merge([arrived[row] for row in range(NY)], 16)
    lse = pltpu.roll(jnp.broadcast_to(lse, (8, HEAD)), HEAD - 16, 1)[0:1]
    packed = pack(average, lse)
    for device in range(GROUP):
        out[device] = packed


def finish_kernel(arrived, out):
    rest = jnp.zeros((HEAD - PACK, HEAD), jnp.bfloat16)
    parts = [jnp.concatenate([arrived[device], rest], axis=0) for device in range(GROUP)]
    out[...] = merge(parts, 0)[0].astype(jnp.bfloat16)


def combine(kernel, shape, arrived):
    return pl.pallas_call(
        kernel,
        out_shape=jax.ShapeDtypeStruct(shape, jnp.bfloat16),
        **params(PACK * HEAD * 32, 1 << 19),
    )(arrived)


def write_kernel(numbers, arrived, cache, new_cache):
    t = numbers[4]
    rows = jnp.concatenate([arrived[(row - FIRST_Y) % NY, :16].astype(jnp.float32) for row in range(NY)], axis=0)
    rows = rows.astype(jnp.bfloat16)
    for conv in range(CONV):
        history, length = numbers[conv], numbers[2 + conv]
        within = (t - history) & (SEQ - 1)
        first = lax.div(history + within, SEQ)
        row = lax.broadcasted_iota(jnp.int32, (LOCAL, HEAD), 0) - first
        column = lax.broadcasted_iota(jnp.int32, (LOCAL, HEAD), 1)
        slot = (column & 3) * NY + (column >> 4)
        live = (((column >> 2) & 1) == conv) & (slot * SEQ + within < length) & (row == slot)
        written = (row >= 0) & (row < 32) & (row * SEQ + within < length)
        for half in range(2):
            place = jnp.where(live & (((column >> 3) & 1) == half), 1.0, 0.0).astype(jnp.bfloat16)
            placed = jnp.dot(place, rows, preferred_element_type=jnp.float32)
            lanes = slice(half * HEAD, half * HEAD + HEAD)
            kept = jnp.where(written, placed, cache[conv, :, lanes].astype(jnp.float32))
            new_cache[conv, :, lanes] = kept.astype(jnp.bfloat16)


def write(numbers, arrived, cache):
    return pl.pallas_call(
        write_kernel,
        in_specs=[SMEM] + [VMEM] * 2,
        out_specs=VMEM,
        out_shape=jax.ShapeDtypeStruct((CONV, LOCAL, FEATURE), jnp.bfloat16),
        **params(4 * CONV * LOCAL * HEAD * FEATURE, 1 << 20),
    )(numbers, arrived, cache)


def on_device(new_hidden, kv_weight, kv_cache, step_kv, queries, hist_len, new_len):
    x, y, core, z = (lax.axis_index(name) for name in ALL)
    t = (x * NY + y) * NC + core
    own = x * NC + core

    weight = exchange(split_weight(kv_weight), ("x", "y", "core"), FIRST_SEQ).reshape(WIDTH, FEATURE)

    swap = [(0, 1), (1, 0)]
    there, back = [], []
    for chip in range(NX):
        for side, step in ((0, NX - 1), (1, 1)):
            there.append((chip * NC + side, (chip + step) % NX * NC + side))
            back.append((chip * NC + side, (chip - step) % NX * NC + side))
    hidden = new_hidden.reshape(CONV * TURN_DEV, WIDTH)
    after = lax.ppermute(hidden, ("x", "core"), there)
    hidden, after = lax.optimization_barrier((hidden, after))
    before = lax.ppermute(hidden, ("x", "core"), back)
    near = jnp.concatenate([hidden, after], axis=0)
    far = jnp.concatenate([before, lax.ppermute(after, ("x", "core"), there)], axis=0)
    near_other = lax.ppermute(near, "core", swap)
    near_other, hist_len, new_len = lax.optimization_barrier((near_other, hist_len, new_len))
    blocks = [near, near_other, far, lax.ppermute(far, "core", swap)]
    numbers = jnp.concatenate([hist_len, new_len, jnp.stack([t, y, own, z])]).astype(jnp.int32)

    def axis(size, place):
        shape = [1, 1, 1, 1]
        shape[place] = size
        return jnp.arange(size, dtype=jnp.int32).reshape(shape)

    history = hist_len.reshape(1, 1, CONV, 1)
    source_x = axis(NX, 3)

    def within_of(device):
        owner = device // NC * (NY * NC) + axis(NY, 1) * NC + device % NC
        return (owner - history) % SEQ

    within = within_of(axis(GROUP, 0))
    crossed = within // TURN_DEV ^ core
    place = jnp.where(within // TURN_DEV == 0, source_x - x, x - source_x) % NX
    place = jnp.where(place < 2, place, 7 - place) + crossed * 2
    column = place * SLICE + axis(CONV, 2) * TURN_DEV + within % TURN_DEV
    order = (column.reshape(ROWS, 1) == jnp.arange(ROWS, dtype=jnp.int32)[None, :]).astype(jnp.bfloat16)

    position = history + (source_x * NY + y) * SEQ + within_of(own)
    frequency = rope_base ** (-2.0 * jnp.arange(HEAD // 2, dtype=jnp.float32) / HEAD)
    angles = position.reshape(SLICE, 1).astype(jnp.float32) * frequency[None, :]
    cosine, sine = jnp.cos(angles), jnp.sin(angles)
    cosine = jnp.concatenate([cosine, cosine], axis=1)
    sine = jnp.concatenate([-sine, sine], axis=1)

    asked = queries.transpose(0, 2, 1, 3).reshape(CONV, QROWS, HEAD)
    steps = jnp.pad(step_kv.reshape(CONV, STEPS, FEATURE), ((0, 0), (0, 16 - STEPS), (0, 0)))
    cache = kv_cache.reshape(CONV, LOCAL, FEATURE)

    partial = exchange(project(numbers, blocks, weight, order), ("kv", "x", "core"), FIRST)
    history_part = attend_history(numbers, cache, steps, asked)
    rows = exchange(attend(numbers, partial, cosine, sine, asked, history_part), ("y",), FIRST_Y)
    packed = exchange(combine(merge_kernel, (GROUP, PACK, HEAD), rows), ("x", "core"), FIRST_GROUP)
    new_cache = write(numbers, rows, cache)
    attended = combine(finish_kernel, (ALL_Q, HEAD), packed)
    attended = attended.reshape(CONV, QPK, STEPS, HEAD).transpose(0, 2, 1, 3)
    return attended, new_cache.reshape(kv_cache.shape)


def solution(mesh):
    split = Mesh(mesh.devices.reshape(NX, NY, NC, NZ), ALL)
    seq = ALL[:3]
    return jax.shard_map(
        on_device,
        mesh=split,
        in_specs=(
            P(None, seq, "kv"),
            P(("kv",) + seq, None),
            P(None, seq, "kv", None),
            P(None, None, "kv", None),
            P(None, None, "kv", None),
            P(),
            P(),
        ),
        out_specs=(P(None, None, "kv", None), P(None, seq, "kv", None)),
        check_vma=False,
    )
```

```python
import jax
import jax.numpy as jnp
from jax import lax
from jax.experimental import pallas as pl
from jax.experimental.pallas import tpu as pltpu
from jax.sharding import Mesh
from jax.sharding import PartitionSpec as P

rope_base = 1000000.0
NX, NY, NC, NZ = 4, 8, 2, 8
SEQ = NX * NY * NC
GROUP = NX * NC
ALL = ("x", "y", "core", "kv")
CONV, TURN_DEV, WIDTH, HEAD, FEATURE = 2, 32, 1536, 128, 256
ROWS, SLICE = 512, 64
LOCAL = 256
STEPS, QPK = 4, 12
QROWS = STEPS * QPK
ALL_Q = CONV * QROWS
PACK = ALL_Q + 16
PIECE = 32
FIRST_SEQ = (2 * NY + 6) * NC
FIRST = 6 * GROUP + 2 * NC
FIRST_Y = 4
FIRST_GROUP = 2 * NC
VMEM_LIMIT = 48 * 1024 * 1024
SMEM = pl.BlockSpec(memory_space=pltpu.SMEM)
VMEM = pl.BlockSpec(memory_space=pltpu.VMEM)


def params(flops, nbytes):
    return dict(
        compiler_params=pltpu.CompilerParams(vmem_limit_bytes=VMEM_LIMIT),
        cost_estimate=pl.CostEstimate(flops=flops, bytes_accessed=nbytes, transcendentals=0),
    )


def exchange(value, names, first=0):
    size = value.shape[0]
    groups = [[(place + first) % size for place in range(size)]] if first else None
    return lax.all_to_all(value, names, split_axis=0, concat_axis=0, tiled=True, axis_index_groups=groups)


def lane_group(rows):
    return lax.broadcasted_iota(jnp.int32, (rows, HEAD), 1) // PIECE


def split_weight_kernel(source, out, weight):
    pltpu.sync_copy(source, weight)
    depth = weight.shape[0]
    group = lane_group(depth)
    for c in range(GROUP):
        tiles = []
        for half in range(2):
            tile = jnp.zeros((depth, HEAD), jnp.float32)
            for head in range(4 * half, 4 * half + 4):
                start = head * FEATURE + c // 4 * HEAD
                columns = weight[:, start : start + HEAD].astype(jnp.float32)
                tile = jnp.where(group == (c + head) % 4, columns, tile)
            tiles.append(tile)
        columns = jnp.concatenate(tiles, axis=1).astype(jnp.bfloat16)
        for y in range(NY):
            out[(c // NC * (NY * NC) + y * NC + c % NC - FIRST_SEQ) % SEQ] = columns


def split_weight(weight):
    depth = weight.shape[0]
    return pl.pallas_call(
        split_weight_kernel,
        in_specs=[pl.BlockSpec(memory_space=pltpu.HBM)],
        scratch_shapes=[pltpu.VMEM(weight.shape, weight.dtype)],
        out_shape=jax.ShapeDtypeStruct((SEQ, depth, FEATURE), jnp.bfloat16),
        **params(1 << 20, 1 << 20),
    )(weight)


def project_kernel(numbers, near, near_other, far, far_other, weight, order, out):
    rows = jnp.concatenate([near[...], near_other[...], far[...], far_other[...]], axis=0)
    start = (SEQ - FIRST_SEQ) * (WIDTH // SEQ)
    weights = jnp.concatenate([weight[start:], weight[:start]], axis=0)
    partial = jnp.dot(rows, weights, preferred_element_type=jnp.float32).astype(jnp.bfloat16)
    half_rows = ROWS // 2
    halves = [
        jnp.dot(order[start : start + half_rows], partial, preferred_element_type=jnp.float32)
        for start in (0, half_rows)
    ]
    own = numbers[6]
    group = lane_group(16)
    for owner in range(GROUP):
        for half in range(2):
            turned = []
            for part in range(4):
                start = owner % (GROUP // 2) * SLICE + part * 16
                tile = halves[owner // (GROUP // 2)][start : start + 16, half * HEAD : half * HEAD + HEAD]
                turned.append(pltpu.roll(tile, part * PIECE, 1) if part else tile)
            for head in range(4 * half, 4 * half + 4):
                message = turned[0]
                for part in range(1, 4):
                    message = jnp.where(group == ((own + head + part) & 3), turned[part], message)
                out[(head * GROUP + owner - FIRST) % (NZ * GROUP)] = message.astype(jnp.bfloat16)


def project(numbers, blocks, weight, order):
    return pl.pallas_call(
        project_kernel,
        in_specs=[SMEM] + [VMEM] * 6,
        out_specs=VMEM,
        out_shape=jax.ShapeDtypeStruct((NZ * GROUP, 16, HEAD), jnp.bfloat16),
        **params(2 * ROWS * WIDTH * FEATURE, 3 << 20),
    )(numbers, *blocks, weight, order)


def pack(average, row):
    high = row.astype(jnp.bfloat16).astype(jnp.float32)
    middle = (row - high).astype(jnp.bfloat16).astype(jnp.float32)
    low = row - high - middle
    place = lax.broadcasted_iota(jnp.int32, (16, HEAD), 0)
    stats = jnp.where(place == 0, high, jnp.where(place == 1, middle, jnp.where(place == 2, low, 0.0)))
    return jnp.concatenate([average, stats], axis=0).astype(jnp.bfloat16)


def diagonal(first):
    row = lax.broadcasted_iota(jnp.int32, (ALL_Q, HEAD), 0)
    return row + first == lax.broadcasted_iota(jnp.int32, (ALL_Q, HEAD), 1)


def merge(parts, first):
    rows = []
    for part in parts:
        stats = part[first + ALL_Q : first + PACK].astype(jnp.float32)
        rows.append(stats[0:1] + stats[1:2] + stats[2:3])
    lses = jnp.concatenate(rows, axis=0)
    top = jnp.max(lses, axis=0, keepdims=True)
    weights = jnp.exp(lses - top)
    total = jnp.sum(weights, axis=0, keepdims=True)
    weights = weights / total
    on_diagonal = diagonal(first)
    summed = jnp.zeros((ALL_Q, HEAD), jnp.float32)
    spread = [
        jnp.where(on_diagonal, weights[index : index + 1], 0.0).astype(jnp.bfloat16)
        for index in range(len(parts))
    ]
    for index in range(0, len(parts), 2):
        pair = jnp.concatenate(spread[index : index + 2], axis=1)
        both = jnp.concatenate(parts[index : index + 2], axis=0)
        summed += jnp.dot(pair, both, preferred_element_type=jnp.float32)
    return summed, top + jnp.log(total)


def history_kernel(numbers, cache, step_kv, queries, summed, tops, totals):
    t = numbers[4]
    for conv in range(CONV):
        history, length = numbers[conv], numbers[2 + conv]
        query = queries[conv]
        keys = [cache[conv, :, :HEAD], step_kv[conv, :, :HEAD]]
        values = [cache[conv, :, HEAD:], step_kv[conv, :, HEAD:]]
        position = lax.broadcasted_iota(jnp.int32, (QROWS, LOCAL), 1) * SEQ + t
        step = lax.broadcasted_iota(jnp.int32, (QROWS, 16), 1)
        asked = lax.broadcasted_iota(jnp.int32, (QROWS, 16), 0) & 3
        visible = [
            position < history,
            (step <= asked) & (((history + length + step) & (SEQ - 1)) == t),
        ]
        scores = [score(query, rows) for rows in keys]
        top = jnp.maximum(*[largest(one, seen) for one, seen in zip(scores, visible)])
        weights = [jnp.where(seen, jnp.exp(one - top), 0.0) for one, seen in zip(scores, visible)]
        total = sum(jnp.sum(weight, axis=1, keepdims=True) for weight in weights)
        rows = slice(conv * QROWS, conv * QROWS + QROWS)
        summed[rows] = sum(blend(weight, value) for weight, value in zip(weights, values))
        tops[rows] = jnp.broadcast_to(top, (QROWS, HEAD))
        totals[rows] = jnp.broadcast_to(total, (QROWS, HEAD))


def score(query, rows):
    contract = (((1,), (1,)), ((), ()))
    return lax.dot_general(query, rows, contract, preferred_element_type=jnp.float32) * HEAD ** (-0.5)


def largest(scores, seen):
    return jnp.max(jnp.where(seen, scores, -3e38), axis=1, keepdims=True)


def blend(weights, rows):
    return jnp.dot(weights.astype(jnp.bfloat16), rows, preferred_element_type=jnp.float32)


def attend_history(numbers, cache, step_kv, queries):
    return pl.pallas_call(
        history_kernel,
        in_specs=[SMEM] + [VMEM] * 3,
        out_specs=[VMEM] * 3,
        out_shape=[jax.ShapeDtypeStruct((ALL_Q, HEAD), jnp.float32)] * 3,
        **params(2 * ALL_Q * LOCAL * FEATURE, 1 << 20),
    )(numbers, cache, step_kv, queries)


def attend_kernel(numbers, arrived, cosine, sine, queries, summed, tops, totals, out):
    y, own, z = numbers[5], numbers[6], numbers[7]
    group = lane_group(16)
    sums = []
    for c in range(GROUP):
        total = arrived[(c - FIRST) % (NZ * GROUP)].astype(jnp.float32)
        for plane in range(1, NZ):
            total += arrived[(plane * GROUP + c - FIRST) % (NZ * GROUP)].astype(jnp.float32)
        sums.append(total)
    halves = []
    for tile in range(2):
        pieces = []
        for part in range(4):
            piece = sums[4 * tile]
            for c in range(4 * tile + 1, 4 * tile + 4):
                piece = jnp.where(group == ((c + z + part) & 3), sums[c], piece)
            pieces.append(pltpu.roll(piece, HEAD - part * PIECE, 1) if part else piece)
        halves.append(jnp.concatenate(pieces, axis=0))
    key, value = halves
    key = key * cosine[...] + pltpu.roll(key, HEAD // 2, 1) * sine[...]
    for row in range(NY):
        both = jnp.concatenate([key[row * 8 : row * 8 + 8], value[row * 8 : row * 8 + 8]], axis=0)
        out[(row - FIRST_Y) % NY, :16] = both.astype(jnp.bfloat16)
    key, value = key.astype(jnp.bfloat16), value.astype(jnp.bfloat16)

    asker = lax.broadcasted_iota(jnp.int32, (ALL_Q, SLICE), 0) >= QROWS
    row = lax.broadcasted_iota(jnp.int32, (ALL_Q, SLICE), 1)
    history = jnp.where(asker, numbers[1], numbers[0])
    length = jnp.where(asker, numbers[3], numbers[2])
    owner = own // NC * (NY * NC) + (row >> 3) * NC + own % NC
    offset = ((row & 3) * NY + y) * SEQ + ((owner - history) & (SEQ - 1))
    visible = (((row >> 2) & 1) == asker.astype(jnp.int32)) & (offset < length)
    scores = score(jnp.concatenate([queries[0], queries[1]], axis=0), key)
    old_top = tops[:, :1]
    top = jnp.maximum(old_top, largest(scores, visible))
    weights = jnp.where(visible, jnp.exp(scores - top), 0.0)
    kept = jnp.exp(old_top - top)
    total = totals[:, :1] * kept + jnp.sum(weights, axis=1, keepdims=True)
    average = (summed[...] * kept + blend(weights, value)) / total
    lse = jnp.sum(jnp.where(diagonal(16), top + jnp.log(total), 0.0), axis=0, keepdims=True)
    packed = pack(average, lse)
    for row in range(NY):
        out[row, 16:] = packed


def attend(numbers, arrived, cosine, sine, queries, history):
    return pl.pallas_call(
        attend_kernel,
        in_specs=[SMEM] + [VMEM] * 7,
        out_specs=VMEM,
        out_shape=jax.ShapeDtypeStruct((NY, 16 + PACK, HEAD), jnp.bfloat16),
        **params(4 * ALL_Q * SLICE * HEAD, 1 << 20),
    )(numbers, arrived, cosine, sine, queries, *history)


def merge_kernel(arrived, out):
    average, lse = merge([arrived[row] for row in range(NY)], 16)
    lse = pltpu.roll(jnp.broadcast_to(lse, (8, HEAD)), HEAD - 16, 1)[0:1]
    packed = pack(average, lse)
    for device in range(GROUP):
        out[device] = packed


def finish_kernel(arrived, out):
    rest = jnp.zeros((HEAD - PACK, HEAD), jnp.bfloat16)
    parts = [jnp.concatenate([arrived[device], rest], axis=0) for device in range(GROUP)]
    out[...] = merge(parts, 0)[0].astype(jnp.bfloat16)


def combine(kernel, shape, arrived):
    return pl.pallas_call(
        kernel,
        out_shape=jax.ShapeDtypeStruct(shape, jnp.bfloat16),
        **params(PACK * HEAD * 32, 1 << 19),
    )(arrived)


def write_kernel(numbers, arrived, cache, new_cache):
    t = numbers[4]
    rows = jnp.concatenate([arrived[(row - FIRST_Y) % NY, :16].astype(jnp.float32) for row in range(NY)], axis=0)
    rows = rows.astype(jnp.bfloat16)
    for conv in range(CONV):
        history, length = numbers[conv], numbers[2 + conv]
        within = (t - history) & (SEQ - 1)
        first = lax.div(history + within, SEQ)
        row = lax.broadcasted_iota(jnp.int32, (LOCAL, HEAD), 0) - first
        column = lax.broadcasted_iota(jnp.int32, (LOCAL, HEAD), 1)
        slot = (column & 3) * NY + (column >> 4)
        live = (((column >> 2) & 1) == conv) & (slot * SEQ + within < length) & (row == slot)
        written = (row >= 0) & (row < 32) & (row * SEQ + within < length)
        for half in range(2):
            place = jnp.where(live & (((column >> 3) & 1) == half), 1.0, 0.0).astype(jnp.bfloat16)
            placed = jnp.dot(place, rows, preferred_element_type=jnp.float32)
            lanes = slice(half * HEAD, half * HEAD + HEAD)
            kept = jnp.where(written, placed, cache[conv, :, lanes].astype(jnp.float32))
            new_cache[conv, :, lanes] = kept.astype(jnp.bfloat16)


def write(numbers, arrived, cache):
    return pl.pallas_call(
        write_kernel,
        in_specs=[SMEM] + [VMEM] * 2,
        out_specs=VMEM,
        out_shape=jax.ShapeDtypeStruct((CONV, LOCAL, FEATURE), jnp.bfloat16),
        **params(4 * CONV * LOCAL * HEAD * FEATURE, 1 << 20),
    )(numbers, arrived, cache)


def on_device(new_hidden, kv_weight, kv_cache, step_kv, queries, hist_len, new_len):
    x, y, core, z = (lax.axis_index(name) for name in ALL)
    t = (x * NY + y) * NC + core
    own = x * NC + core

    weight = exchange(split_weight(kv_weight), ("x", "y", "core"), FIRST_SEQ).reshape(WIDTH, FEATURE)

    swap = [(0, 1), (1, 0)]
    there, back = [], []
    for chip in range(NX):
        for side, step in ((0, NX - 1), (1, 1)):
            there.append((chip * NC + side, (chip + step) % NX * NC + side))
            back.append((chip * NC + side, (chip - step) % NX * NC + side))
    hidden = new_hidden.reshape(CONV * TURN_DEV, WIDTH)
    after = lax.ppermute(hidden, ("x", "core"), there)
    hidden, after = lax.optimization_barrier((hidden, after))
    before = lax.ppermute(hidden, ("x", "core"), back)
    near = jnp.concatenate([hidden, after], axis=0)
    far = jnp.concatenate([before, lax.ppermute(after, ("x", "core"), there)], axis=0)
    near_other = lax.ppermute(near, "core", swap)
    near_other, hist_len, new_len = lax.optimization_barrier((near_other, hist_len, new_len))
    blocks = [near, near_other, far, lax.ppermute(far, "core", swap)]
    numbers = jnp.concatenate([hist_len, new_len, jnp.stack([t, y, own, z])]).astype(jnp.int32)

    def axis(size, place):
        shape = [1, 1, 1, 1]
        shape[place] = size
        return jnp.arange(size, dtype=jnp.int32).reshape(shape)

    history = hist_len.reshape(1, 1, CONV, 1)
    source_x = axis(NX, 3)

    def within_of(device):
        owner = device // NC * (NY * NC) + axis(NY, 1) * NC + device % NC
        return (owner - history) % SEQ

    within = within_of(axis(GROUP, 0))
    crossed = within // TURN_DEV ^ core
    place = jnp.where(within // TURN_DEV == 0, source_x - x, x - source_x) % NX
    place = jnp.where(place < 2, place, 7 - place) + crossed * 2
    column = place * SLICE + axis(CONV, 2) * TURN_DEV + within % TURN_DEV
    order = (column.reshape(ROWS, 1) == jnp.arange(ROWS, dtype=jnp.int32)[None, :]).astype(jnp.bfloat16)

    position = history + (source_x * NY + y) * SEQ + within_of(own)
    frequency = rope_base ** (-2.0 * jnp.arange(HEAD // 2, dtype=jnp.float32) / HEAD)
    angles = position.reshape(SLICE, 1).astype(jnp.float32) * frequency[None, :]
    cosine, sine = jnp.cos(angles), jnp.sin(angles)
    cosine = jnp.concatenate([cosine, cosine], axis=1)
    sine = jnp.concatenate([-sine, sine], axis=1)

    asked = queries.transpose(0, 2, 1, 3).reshape(CONV, QROWS, HEAD)
    steps = jnp.pad(step_kv.reshape(CONV, STEPS, FEATURE), ((0, 0), (0, 16 - STEPS), (0, 0)))
    cache = kv_cache.reshape(CONV, LOCAL, FEATURE)

    history_part = attend_history(numbers, cache, steps, asked)
    order, cosine, sine, asked, history_part = lax.optimization_barrier(
        (order, cosine, sine, asked, history_part)
    )
    partial = exchange(project(numbers, blocks, weight, order), ("kv", "x", "core"), FIRST)
    rows = exchange(attend(numbers, partial, cosine, sine, asked, history_part), ("y",), FIRST_Y)
    packed = exchange(combine(merge_kernel, (GROUP, PACK, HEAD), rows), ("x", "core"), FIRST_GROUP)
    new_cache = write(numbers, rows, cache)
    attended = combine(finish_kernel, (ALL_Q, HEAD), packed)
    attended = attended.reshape(CONV, QPK, STEPS, HEAD).transpose(0, 2, 1, 3)
    return attended, new_cache.reshape(kv_cache.shape)


def solution(mesh):
    split = Mesh(mesh.devices.reshape(NX, NY, NC, NZ), ALL)
    seq = ALL[:3]
    return jax.shard_map(
        on_device,
        mesh=split,
        in_specs=(
            P(None, seq, "kv"),
            P(("kv",) + seq, None),
            P(None, seq, "kv", None),
            P(None, None, "kv", None),
            P(None, None, "kv", None),
            P(),
            P(),
        ),
        out_specs=(P(None, None, "kv", None), P(None, seq, "kv", None)),
        check_vma=False,
    )
```

```python
import jax
import jax.numpy as jnp
from jax import lax
from jax.experimental import pallas as pl
from jax.experimental.pallas import tpu as pltpu
from jax.sharding import Mesh
from jax.sharding import PartitionSpec as P

rope_base = 1000000.0
NX, NY, NC, NZ = 4, 8, 2, 8
SEQ = NX * NY * NC
GROUP = NX * NC
ALL = ("x", "y", "core", "kv")
CONV, TURN_DEV, WIDTH, HEAD, FEATURE = 2, 32, 1536, 128, 256
ROWS, SLICE = 512, 64
LOCAL = 256
STEPS, QPK = 4, 12
QROWS = STEPS * QPK
ALL_Q = CONV * QROWS
PACK = ALL_Q + 16
PIECE = 32
FIRST_SEQ = (2 * NY + 6) * NC
FIRST = 6 * GROUP + 2 * NC
FIRST_Y = 4
FIRST_GROUP = 2 * NC
VMEM_LIMIT = 48 * 1024 * 1024
SMEM = pl.BlockSpec(memory_space=pltpu.SMEM)
VMEM = pl.BlockSpec(memory_space=pltpu.VMEM)


def params(flops, nbytes):
    return dict(
        compiler_params=pltpu.CompilerParams(vmem_limit_bytes=VMEM_LIMIT),
        cost_estimate=pl.CostEstimate(flops=flops, bytes_accessed=nbytes, transcendentals=0),
    )


def exchange(value, names, first=0):
    size = value.shape[0]
    groups = [[(place + first) % size for place in range(size)]] if first else None
    return lax.all_to_all(value, names, split_axis=0, concat_axis=0, tiled=True, axis_index_groups=groups)


def lane_group(rows):
    return lax.broadcasted_iota(jnp.int32, (rows, HEAD), 1) // PIECE


def split_weight_kernel(source, out, weight):
    pltpu.sync_copy(source, weight)
    depth = weight.shape[0]
    group = lane_group(depth)
    for c in range(GROUP):
        tiles = []
        for half in range(2):
            tile = jnp.zeros((depth, HEAD), jnp.float32)
            for head in range(4 * half, 4 * half + 4):
                start = head * FEATURE + c // 4 * HEAD
                columns = weight[:, start : start + HEAD].astype(jnp.float32)
                tile = jnp.where(group == (c + head) % 4, columns, tile)
            tiles.append(tile)
        columns = jnp.concatenate(tiles, axis=1).astype(jnp.bfloat16)
        for y in range(NY):
            out[(c // NC * (NY * NC) + y * NC + c % NC - FIRST_SEQ) % SEQ] = columns


def split_weight(weight):
    depth = weight.shape[0]
    return pl.pallas_call(
        split_weight_kernel,
        in_specs=[pl.BlockSpec(memory_space=pltpu.HBM)],
        scratch_shapes=[pltpu.VMEM(weight.shape, weight.dtype)],
        out_shape=jax.ShapeDtypeStruct((SEQ, depth, FEATURE), jnp.bfloat16),
        **params(1 << 20, 1 << 20),
    )(weight)


def project_kernel(numbers, near, near_other, far, far_other, weight, order, out):
    rows = jnp.concatenate([near[...], near_other[...], far[...], far_other[...]], axis=0)
    start = (SEQ - FIRST_SEQ) * (WIDTH // SEQ)
    weights = jnp.concatenate([weight[start:], weight[:start]], axis=0)
    partial = jnp.dot(rows, weights, preferred_element_type=jnp.float32).astype(jnp.bfloat16)
    half_rows = ROWS // 2
    halves = [
        jnp.dot(order[start : start + half_rows], partial, preferred_element_type=jnp.float32)
        for start in (0, half_rows)
    ]
    own = numbers[6]
    group = lane_group(16)
    for owner in range(GROUP):
        for half in range(2):
            turned = []
            for part in range(4):
                start = owner % (GROUP // 2) * SLICE + part * 16
                tile = halves[owner // (GROUP // 2)][start : start + 16, half * HEAD : half * HEAD + HEAD]
                turned.append(pltpu.roll(tile, part * PIECE, 1) if part else tile)
            for head in range(4 * half, 4 * half + 4):
                message = turned[0]
                for part in range(1, 4):
                    message = jnp.where(group == ((own + head + part) & 3), turned[part], message)
                out[(head * GROUP + owner - FIRST) % (NZ * GROUP)] = message.astype(jnp.bfloat16)


def project(numbers, blocks, weight, order):
    return pl.pallas_call(
        project_kernel,
        in_specs=[SMEM] + [VMEM] * 6,
        out_specs=VMEM,
        out_shape=jax.ShapeDtypeStruct((NZ * GROUP, 16, HEAD), jnp.bfloat16),
        **params(2 * ROWS * WIDTH * FEATURE, 3 << 20),
    )(numbers, *blocks, weight, order)


def pack(average, row):
    high = row.astype(jnp.bfloat16).astype(jnp.float32)
    middle = (row - high).astype(jnp.bfloat16).astype(jnp.float32)
    low = row - high - middle
    place = lax.broadcasted_iota(jnp.int32, (16, HEAD), 0)
    stats = jnp.where(place == 0, high, jnp.where(place == 1, middle, jnp.where(place == 2, low, 0.0)))
    return jnp.concatenate([average, stats], axis=0).astype(jnp.bfloat16)


def diagonal(first):
    row = lax.broadcasted_iota(jnp.int32, (ALL_Q, HEAD), 0)
    return row + first == lax.broadcasted_iota(jnp.int32, (ALL_Q, HEAD), 1)


def merge(parts, first):
    rows = []
    for part in parts:
        stats = part[first + ALL_Q : first + PACK].astype(jnp.float32)
        rows.append(stats[0:1] + stats[1:2] + stats[2:3])
    lses = jnp.concatenate(rows, axis=0)
    top = jnp.max(lses, axis=0, keepdims=True)
    weights = jnp.exp(lses - top)
    total = jnp.sum(weights, axis=0, keepdims=True)
    weights = weights / total
    on_diagonal = diagonal(first)
    summed = jnp.zeros((ALL_Q, HEAD), jnp.float32)
    spread = [
        jnp.where(on_diagonal, weights[index : index + 1], 0.0).astype(jnp.bfloat16)
        for index in range(len(parts))
    ]
    for index in range(0, len(parts), 2):
        pair = jnp.concatenate(spread[index : index + 2], axis=1)
        both = jnp.concatenate(parts[index : index + 2], axis=0)
        summed += jnp.dot(pair, both, preferred_element_type=jnp.float32)
    return summed, top + jnp.log(total)


def history_kernel(numbers, cache, step_kv, queries, summed, tops, totals):
    t = numbers[4]
    for conv in range(CONV):
        history, length = numbers[conv], numbers[2 + conv]
        query = queries[conv]
        keys = [cache[conv, :, :HEAD], step_kv[conv, :, :HEAD]]
        values = [cache[conv, :, HEAD:], step_kv[conv, :, HEAD:]]
        position = lax.broadcasted_iota(jnp.int32, (QROWS, LOCAL), 1) * SEQ + t
        step = lax.broadcasted_iota(jnp.int32, (QROWS, 16), 1)
        asked = lax.broadcasted_iota(jnp.int32, (QROWS, 16), 0) & 3
        visible = [
            position < history,
            (step <= asked) & (((history + length + step) & (SEQ - 1)) == t),
        ]
        scores = [score(query, rows) for rows in keys]
        top = jnp.maximum(*[largest(one, seen) for one, seen in zip(scores, visible)])
        weights = [jnp.where(seen, jnp.exp(one - top), 0.0) for one, seen in zip(scores, visible)]
        total = sum(jnp.sum(weight, axis=1, keepdims=True) for weight in weights)
        rows = slice(conv * QROWS, conv * QROWS + QROWS)
        summed[rows] = sum(blend(weight, value) for weight, value in zip(weights, values))
        tops[rows] = jnp.broadcast_to(top, (QROWS, HEAD))
        totals[rows] = jnp.broadcast_to(total, (QROWS, HEAD))


def score(query, rows):
    contract = (((1,), (1,)), ((), ()))
    return lax.dot_general(query, rows, contract, preferred_element_type=jnp.float32) * HEAD ** (-0.5)


def largest(scores, seen):
    return jnp.max(jnp.where(seen, scores, -3e38), axis=1, keepdims=True)


def blend(weights, rows):
    return jnp.dot(weights.astype(jnp.bfloat16), rows, preferred_element_type=jnp.float32)


def attend_history(numbers, cache, step_kv, queries):
    return pl.pallas_call(
        history_kernel,
        in_specs=[SMEM] + [VMEM] * 3,
        out_specs=[VMEM] * 3,
        out_shape=[jax.ShapeDtypeStruct((ALL_Q, HEAD), jnp.float32)] * 3,
        **params(2 * ALL_Q * LOCAL * FEATURE, 1 << 20),
    )(numbers, cache, step_kv, queries)


def attend_kernel(numbers, arrived, cosine, sine, queries, summed, tops, totals, out):
    y, own, z = numbers[5], numbers[6], numbers[7]
    group = lane_group(16)
    sums = []
    for c in range(GROUP):
        total = arrived[(c - FIRST) % (NZ * GROUP)].astype(jnp.float32)
        for plane in range(1, NZ):
            total += arrived[(plane * GROUP + c - FIRST) % (NZ * GROUP)].astype(jnp.float32)
        sums.append(total)
    halves = []
    for tile in range(2):
        pieces = []
        for part in range(4):
            piece = sums[4 * tile]
            for c in range(4 * tile + 1, 4 * tile + 4):
                piece = jnp.where(group == ((c + z + part) & 3), sums[c], piece)
            pieces.append(pltpu.roll(piece, HEAD - part * PIECE, 1) if part else piece)
        halves.append(jnp.concatenate(pieces, axis=0))
    key, value = halves
    key = key * cosine[...] + pltpu.roll(key, HEAD // 2, 1) * sine[...]
    for row in range(NY):
        both = jnp.concatenate([key[row * 8 : row * 8 + 8], value[row * 8 : row * 8 + 8]], axis=0)
        out[(row - FIRST_Y) % NY, :16] = both.astype(jnp.bfloat16)
    key, value = key.astype(jnp.bfloat16), value.astype(jnp.bfloat16)

    asker = lax.broadcasted_iota(jnp.int32, (ALL_Q, SLICE), 0) >= QROWS
    row = lax.broadcasted_iota(jnp.int32, (ALL_Q, SLICE), 1)
    history = jnp.where(asker, numbers[1], numbers[0])
    length = jnp.where(asker, numbers[3], numbers[2])
    owner = own // NC * (NY * NC) + (row >> 3) * NC + own % NC
    offset = ((row & 3) * NY + y) * SEQ + ((owner - history) & (SEQ - 1))
    visible = (((row >> 2) & 1) == asker.astype(jnp.int32)) & (offset < length)
    scores = score(jnp.concatenate([queries[0], queries[1]], axis=0), key)
    old_top = tops[:, :1]
    top = jnp.maximum(old_top, largest(scores, visible))
    weights = jnp.where(visible, jnp.exp(scores - top), 0.0)
    kept = jnp.exp(old_top - top)
    total = totals[:, :1] * kept + jnp.sum(weights, axis=1, keepdims=True)
    average = (summed[...] * kept + blend(weights, value)) / total
    lse = jnp.sum(jnp.where(diagonal(16), top + jnp.log(total), 0.0), axis=0, keepdims=True)
    packed = pack(average, lse)
    for row in range(NY):
        out[row, 16:] = packed


def attend(numbers, arrived, cosine, sine, queries, history):
    return pl.pallas_call(
        attend_kernel,
        in_specs=[SMEM] + [VMEM] * 7,
        out_specs=VMEM,
        out_shape=jax.ShapeDtypeStruct((NY, 16 + PACK, HEAD), jnp.bfloat16),
        **params(4 * ALL_Q * SLICE * HEAD, 1 << 20),
    )(numbers, arrived, cosine, sine, queries, *history)


def merge_kernel(arrived, out):
    average, lse = merge([arrived[row] for row in range(NY)], 16)
    lse = pltpu.roll(jnp.broadcast_to(lse, (8, HEAD)), HEAD - 16, 1)[0:1]
    packed = pack(average, lse)
    for device in range(GROUP):
        out[device] = packed


def finish_kernel(arrived, out):
    rest = jnp.zeros((HEAD - PACK, HEAD), jnp.bfloat16)
    parts = [jnp.concatenate([arrived[device], rest], axis=0) for device in range(GROUP)]
    out[...] = merge(parts, 0)[0].astype(jnp.bfloat16)


def combine(kernel, shape, arrived):
    return pl.pallas_call(
        kernel,
        out_shape=jax.ShapeDtypeStruct(shape, jnp.bfloat16),
        **params(PACK * HEAD * 32, 1 << 19),
    )(arrived)


def write_kernel(numbers, arrived, cache, new_cache):
    t = numbers[4]
    rows = jnp.concatenate([arrived[(row - FIRST_Y) % NY, :16].astype(jnp.float32) for row in range(NY)], axis=0)
    rows = rows.astype(jnp.bfloat16)
    for conv in range(CONV):
        history, length = numbers[conv], numbers[2 + conv]
        within = (t - history) & (SEQ - 1)
        first = lax.div(history + within, SEQ)
        row = lax.broadcasted_iota(jnp.int32, (LOCAL, HEAD), 0) - first
        column = lax.broadcasted_iota(jnp.int32, (LOCAL, HEAD), 1)
        slot = (column & 3) * NY + (column >> 4)
        live = (((column >> 2) & 1) == conv) & (slot * SEQ + within < length) & (row == slot)
        written = (row >= 0) & (row < 32) & (row * SEQ + within < length)
        for half in range(2):
            place = jnp.where(live & (((column >> 3) & 1) == half), 1.0, 0.0).astype(jnp.bfloat16)
            placed = jnp.dot(place, rows, preferred_element_type=jnp.float32)
            lanes = slice(half * HEAD, half * HEAD + HEAD)
            kept = jnp.where(written, placed, cache[conv, :, lanes].astype(jnp.float32))
            new_cache[conv, :, lanes] = kept.astype(jnp.bfloat16)


def write(numbers, arrived, cache):
    return pl.pallas_call(
        write_kernel,
        in_specs=[SMEM] + [VMEM] * 2,
        out_specs=VMEM,
        out_shape=jax.ShapeDtypeStruct((CONV, LOCAL, FEATURE), jnp.bfloat16),
        **params(4 * CONV * LOCAL * HEAD * FEATURE, 1 << 20),
    )(numbers, arrived, cache)


def on_device(new_hidden, kv_weight, kv_cache, step_kv, queries, hist_len, new_len):
    x, y, core, z = (lax.axis_index(name) for name in ALL)
    t = (x * NY + y) * NC + core
    own = x * NC + core

    weight = exchange(split_weight(kv_weight), ("x", "y", "core"), FIRST_SEQ).reshape(WIDTH, FEATURE)

    swap = [(0, 1), (1, 0)]
    there, back = [], []
    for chip in range(NX):
        for side, step in ((0, NX - 1), (1, 1)):
            there.append((chip * NC + side, (chip + step) % NX * NC + side))
            back.append((chip * NC + side, (chip - step) % NX * NC + side))
    hidden = new_hidden.reshape(CONV * TURN_DEV, WIDTH)
    after = lax.ppermute(hidden, ("x", "core"), there)
    hidden, after = lax.optimization_barrier((hidden, after))
    before = lax.ppermute(hidden, ("x", "core"), back)
    near = jnp.concatenate([hidden, after], axis=0)
    far = jnp.concatenate([before, lax.ppermute(after, ("x", "core"), there)], axis=0)
    near_other = lax.ppermute(near, "core", swap)
    near_other, hist_len, new_len = lax.optimization_barrier((near_other, hist_len, new_len))
    numbers = jnp.concatenate([hist_len, new_len, jnp.stack([t, y, own, z])]).astype(jnp.int32)
    asked = queries.transpose(0, 2, 1, 3).reshape(CONV, QROWS, HEAD)
    steps = jnp.pad(step_kv.reshape(CONV, STEPS, FEATURE), ((0, 0), (0, 16 - STEPS), (0, 0)))
    cache = kv_cache.reshape(CONV, LOCAL, FEATURE)
    history_part = attend_history(numbers, cache, steps, asked)
    far, history_part = lax.optimization_barrier((far, history_part))
    blocks = [near, near_other, far, lax.ppermute(far, "core", swap)]

    def axis(size, place):
        shape = [1, 1, 1, 1]
        shape[place] = size
        return jnp.arange(size, dtype=jnp.int32).reshape(shape)

    history = hist_len.reshape(1, 1, CONV, 1)
    source_x = axis(NX, 3)

    def within_of(device):
        owner = device // NC * (NY * NC) + axis(NY, 1) * NC + device % NC
        return (owner - history) % SEQ

    within = within_of(axis(GROUP, 0))
    crossed = within // TURN_DEV ^ core
    place = jnp.where(within // TURN_DEV == 0, source_x - x, x - source_x) % NX
    place = jnp.where(place < 2, place, 7 - place) + crossed * 2
    column = place * SLICE + axis(CONV, 2) * TURN_DEV + within % TURN_DEV
    order = (column.reshape(ROWS, 1) == jnp.arange(ROWS, dtype=jnp.int32)[None, :]).astype(jnp.bfloat16)

    position = history + (source_x * NY + y) * SEQ + within_of(own)
    frequency = rope_base ** (-2.0 * jnp.arange(HEAD // 2, dtype=jnp.float32) / HEAD)
    angles = position.reshape(SLICE, 1).astype(jnp.float32) * frequency[None, :]
    cosine, sine = jnp.cos(angles), jnp.sin(angles)
    cosine = jnp.concatenate([cosine, cosine], axis=1)
    sine = jnp.concatenate([-sine, sine], axis=1)

    order, cosine, sine, asked = lax.optimization_barrier((order, cosine, sine, asked))
    partial = exchange(project(numbers, blocks, weight, order), ("kv", "x", "core"), FIRST)
    rows = exchange(attend(numbers, partial, cosine, sine, asked, history_part), ("y",), FIRST_Y)
    packed = exchange(combine(merge_kernel, (GROUP, PACK, HEAD), rows), ("x", "core"), FIRST_GROUP)
    new_cache = write(numbers, rows, cache)
    attended = combine(finish_kernel, (ALL_Q, HEAD), packed)
    attended = attended.reshape(CONV, QPK, STEPS, HEAD).transpose(0, 2, 1, 3)
    return attended, new_cache.reshape(kv_cache.shape)


def solution(mesh):
    split = Mesh(mesh.devices.reshape(NX, NY, NC, NZ), ALL)
    seq = ALL[:3]
    return jax.shard_map(
        on_device,
        mesh=split,
        in_specs=(
            P(None, seq, "kv"),
            P(("kv",) + seq, None),
            P(None, seq, "kv", None),
            P(None, None, "kv", None),
            P(None, None, "kv", None),
            P(),
            P(),
        ),
        out_specs=(P(None, None, "kv", None), P(None, seq, "kv", None)),
        check_vma=False,
    )
```

```python
import jax
import jax.numpy as jnp
from jax import lax
from jax.experimental import pallas as pl
from jax.experimental.pallas import tpu as pltpu
from jax.sharding import Mesh
from jax.sharding import PartitionSpec as P

rope_base = 1000000.0
NX, NY, NC, NZ = 4, 8, 2, 8
SEQ = NX * NY * NC
GROUP = NX * NC
ALL = ("x", "y", "core", "kv")
CONV, TURN_DEV, WIDTH, HEAD, FEATURE = 2, 32, 1536, 128, 256
ROWS, SLICE = 512, 64
LOCAL = 256
STEPS, QPK = 4, 12
QROWS = STEPS * QPK
ALL_Q = CONV * QROWS
PACK = ALL_Q + 16
PIECE = 32
SEQ_ORDER = [(2 * NY + 6 + 11 * place) % (NX * NY) * NC + core for place in range(NX * NY) for core in range(NC)]
SUM_ORDER = [(6 * GROUP + 2 * NC + 11 * place) % (NZ * GROUP) for place in range(NZ * GROUP)]
Y_ORDER = [(4 + 3 * place) % NY for place in range(NY)]
GROUP_ORDER = [(2 * NC + place) % GROUP for place in range(GROUP)]
VMEM_LIMIT = 48 * 1024 * 1024
SMEM = pl.BlockSpec(memory_space=pltpu.SMEM)
VMEM = pl.BlockSpec(memory_space=pltpu.VMEM)


def params(flops, nbytes):
    return dict(
        compiler_params=pltpu.CompilerParams(vmem_limit_bytes=VMEM_LIMIT),
        cost_estimate=pl.CostEstimate(flops=flops, bytes_accessed=nbytes, transcendentals=0),
    )


def exchange(value, names, order):
    return lax.all_to_all(value, names, split_axis=0, concat_axis=0, tiled=True, axis_index_groups=[order])


def lane_group(rows):
    return lax.broadcasted_iota(jnp.int32, (rows, HEAD), 1) // PIECE


def split_weight_kernel(source, out, weight):
    pltpu.sync_copy(source, weight)
    depth = weight.shape[0]
    group = lane_group(depth)
    for c in range(GROUP):
        tiles = []
        for half in range(2):
            tile = jnp.zeros((depth, HEAD), jnp.float32)
            for head in range(4 * half, 4 * half + 4):
                start = head * FEATURE + c // 4 * HEAD
                columns = weight[:, start : start + HEAD].astype(jnp.float32)
                tile = jnp.where(group == (c + head) % 4, columns, tile)
            tiles.append(tile)
        columns = jnp.concatenate(tiles, axis=1).astype(jnp.bfloat16)
        for y in range(NY):
            out[SEQ_ORDER.index(c // NC * (NY * NC) + y * NC + c % NC)] = columns


def split_weight(weight):
    depth = weight.shape[0]
    return pl.pallas_call(
        split_weight_kernel,
        in_specs=[pl.BlockSpec(memory_space=pltpu.HBM)],
        scratch_shapes=[pltpu.VMEM(weight.shape, weight.dtype)],
        out_shape=jax.ShapeDtypeStruct((SEQ, depth, FEATURE), jnp.bfloat16),
        **params(1 << 20, 1 << 20),
    )(weight)


def project_kernel(numbers, near, near_other, far, far_other, weight, order, out):
    rows = jnp.concatenate([near[...], near_other[...], far[...], far_other[...]], axis=0)
    run = WIDTH // (NX * NY)
    starts = [SEQ_ORDER.index(chip * NC) // NC * run for chip in range(NX * NY)]
    weights = jnp.concatenate([weight[start : start + run] for start in starts], axis=0)
    partial = jnp.dot(rows, weights, preferred_element_type=jnp.float32).astype(jnp.bfloat16)
    half_rows = ROWS // 2
    halves = [
        jnp.dot(order[start : start + half_rows], partial, preferred_element_type=jnp.float32)
        for start in (0, half_rows)
    ]
    own = numbers[6]
    group = lane_group(16)
    for owner in range(GROUP):
        for half in range(2):
            turned = []
            for part in range(4):
                start = owner % (GROUP // 2) * SLICE + part * 16
                tile = halves[owner // (GROUP // 2)][start : start + 16, half * HEAD : half * HEAD + HEAD]
                turned.append(pltpu.roll(tile, part * PIECE, 1) if part else tile)
            for head in range(4 * half, 4 * half + 4):
                message = turned[0]
                for part in range(1, 4):
                    message = jnp.where(group == ((own + head + part) & 3), turned[part], message)
                out[SUM_ORDER.index(head * GROUP + owner)] = message.astype(jnp.bfloat16)


def project(numbers, blocks, weight, order):
    return pl.pallas_call(
        project_kernel,
        in_specs=[SMEM] + [VMEM] * 6,
        out_specs=VMEM,
        out_shape=jax.ShapeDtypeStruct((NZ * GROUP, 16, HEAD), jnp.bfloat16),
        **params(2 * ROWS * WIDTH * FEATURE, 3 << 20),
    )(numbers, *blocks, weight, order)


def pack(average, row):
    high = row.astype(jnp.bfloat16).astype(jnp.float32)
    middle = (row - high).astype(jnp.bfloat16).astype(jnp.float32)
    low = row - high - middle
    place = lax.broadcasted_iota(jnp.int32, (16, HEAD), 0)
    stats = jnp.where(place == 0, high, jnp.where(place == 1, middle, jnp.where(place == 2, low, 0.0)))
    return jnp.concatenate([average, stats], axis=0).astype(jnp.bfloat16)


def diagonal(first):
    row = lax.broadcasted_iota(jnp.int32, (ALL_Q, HEAD), 0)
    return row + first == lax.broadcasted_iota(jnp.int32, (ALL_Q, HEAD), 1)


def merge(parts, first):
    rows = []
    for part in parts:
        stats = part[first + ALL_Q : first + PACK].astype(jnp.float32)
        rows.append(stats[0:1] + stats[1:2] + stats[2:3])
    lses = jnp.concatenate(rows, axis=0)
    top = jnp.max(lses, axis=0, keepdims=True)
    weights = jnp.exp(lses - top)
    total = jnp.sum(weights, axis=0, keepdims=True)
    weights = weights / total
    on_diagonal = diagonal(first)
    summed = jnp.zeros((ALL_Q, HEAD), jnp.float32)
    spread = [
        jnp.where(on_diagonal, weights[index : index + 1], 0.0).astype(jnp.bfloat16)
        for index in range(len(parts))
    ]
    for index in range(0, len(parts), 2):
        pair = jnp.concatenate(spread[index : index + 2], axis=1)
        both = jnp.concatenate(parts[index : index + 2], axis=0)
        summed += jnp.dot(pair, both, preferred_element_type=jnp.float32)
    return summed, top + jnp.log(total)


def history_kernel(numbers, cache, step_kv, queries, summed, tops, totals):
    t = numbers[4]
    for conv in range(CONV):
        history, length = numbers[conv], numbers[2 + conv]
        query = queries[conv]
        keys = [cache[conv, :, :HEAD], step_kv[conv, :, :HEAD]]
        values = [cache[conv, :, HEAD:], step_kv[conv, :, HEAD:]]
        position = lax.broadcasted_iota(jnp.int32, (QROWS, LOCAL), 1) * SEQ + t
        step = lax.broadcasted_iota(jnp.int32, (QROWS, 16), 1)
        asked = lax.broadcasted_iota(jnp.int32, (QROWS, 16), 0) & 3
        visible = [
            position < history,
            (step <= asked) & (((history + length + step) & (SEQ - 1)) == t),
        ]
        scores = [score(query, rows) for rows in keys]
        top = jnp.maximum(*[largest(one, seen) for one, seen in zip(scores, visible)])
        weights = [jnp.where(seen, jnp.exp(one - top), 0.0) for one, seen in zip(scores, visible)]
        total = sum(jnp.sum(weight, axis=1, keepdims=True) for weight in weights)
        rows = slice(conv * QROWS, conv * QROWS + QROWS)
        summed[rows] = sum(blend(weight, value) for weight, value in zip(weights, values))
        tops[rows] = jnp.broadcast_to(top, (QROWS, HEAD))
        totals[rows] = jnp.broadcast_to(total, (QROWS, HEAD))


def score(query, rows):
    contract = (((1,), (1,)), ((), ()))
    return lax.dot_general(query, rows, contract, preferred_element_type=jnp.float32) * HEAD ** (-0.5)


def largest(scores, seen):
    return jnp.max(jnp.where(seen, scores, -3e38), axis=1, keepdims=True)


def blend(weights, rows):
    return jnp.dot(weights.astype(jnp.bfloat16), rows, preferred_element_type=jnp.float32)


def attend_history(numbers, cache, step_kv, queries):
    return pl.pallas_call(
        history_kernel,
        in_specs=[SMEM] + [VMEM] * 3,
        out_specs=[VMEM] * 3,
        out_shape=[jax.ShapeDtypeStruct((ALL_Q, HEAD), jnp.float32)] * 3,
        **params(2 * ALL_Q * LOCAL * FEATURE, 1 << 20),
    )(numbers, cache, step_kv, queries)


def attend_kernel(numbers, arrived, cosine, sine, queries, summed, tops, totals, out):
    y, own, z = numbers[5], numbers[6], numbers[7]
    group = lane_group(16)
    sums = []
    for c in range(GROUP):
        total = arrived[SUM_ORDER.index(c)].astype(jnp.float32)
        for plane in range(1, NZ):
            total += arrived[SUM_ORDER.index(plane * GROUP + c)].astype(jnp.float32)
        sums.append(total)
    halves = []
    for tile in range(2):
        pieces = []
        for part in range(4):
            piece = sums[4 * tile]
            for c in range(4 * tile + 1, 4 * tile + 4):
                piece = jnp.where(group == ((c + z + part) & 3), sums[c], piece)
            pieces.append(pltpu.roll(piece, HEAD - part * PIECE, 1) if part else piece)
        halves.append(jnp.concatenate(pieces, axis=0))
    key, value = halves
    key = key * cosine[...] + pltpu.roll(key, HEAD // 2, 1) * sine[...]
    for row in range(NY):
        both = jnp.concatenate([key[row * 8 : row * 8 + 8], value[row * 8 : row * 8 + 8]], axis=0)
        out[Y_ORDER.index(row), :16] = both.astype(jnp.bfloat16)
    key, value = key.astype(jnp.bfloat16), value.astype(jnp.bfloat16)

    asker = lax.broadcasted_iota(jnp.int32, (ALL_Q, SLICE), 0) >= QROWS
    row = lax.broadcasted_iota(jnp.int32, (ALL_Q, SLICE), 1)
    history = jnp.where(asker, numbers[1], numbers[0])
    length = jnp.where(asker, numbers[3], numbers[2])
    owner = own // NC * (NY * NC) + (row >> 3) * NC + own % NC
    offset = ((row & 3) * NY + y) * SEQ + ((owner - history) & (SEQ - 1))
    visible = (((row >> 2) & 1) == asker.astype(jnp.int32)) & (offset < length)
    scores = score(jnp.concatenate([queries[0], queries[1]], axis=0), key)
    old_top = tops[:, :1]
    top = jnp.maximum(old_top, largest(scores, visible))
    weights = jnp.where(visible, jnp.exp(scores - top), 0.0)
    kept = jnp.exp(old_top - top)
    total = totals[:, :1] * kept + jnp.sum(weights, axis=1, keepdims=True)
    average = (summed[...] * kept + blend(weights, value)) / total
    lse = jnp.sum(jnp.where(diagonal(16), top + jnp.log(total), 0.0), axis=0, keepdims=True)
    packed = pack(average, lse)
    for row in range(NY):
        out[row, 16:] = packed


def attend(numbers, arrived, cosine, sine, queries, history):
    return pl.pallas_call(
        attend_kernel,
        in_specs=[SMEM] + [VMEM] * 7,
        out_specs=VMEM,
        out_shape=jax.ShapeDtypeStruct((NY, 16 + PACK, HEAD), jnp.bfloat16),
        **params(4 * ALL_Q * SLICE * HEAD, 1 << 20),
    )(numbers, arrived, cosine, sine, queries, *history)


def merge_kernel(arrived, out):
    average, lse = merge([arrived[row] for row in range(NY)], 16)
    lse = pltpu.roll(jnp.broadcast_to(lse, (8, HEAD)), HEAD - 16, 1)[0:1]
    packed = pack(average, lse)
    for device in range(GROUP):
        out[device] = packed


def finish_kernel(arrived, out):
    rest = jnp.zeros((HEAD - PACK, HEAD), jnp.bfloat16)
    parts = [jnp.concatenate([arrived[device], rest], axis=0) for device in range(GROUP)]
    out[...] = merge(parts, 0)[0].astype(jnp.bfloat16)


def combine(kernel, shape, arrived):
    return pl.pallas_call(
        kernel,
        out_shape=jax.ShapeDtypeStruct(shape, jnp.bfloat16),
        **params(PACK * HEAD * 32, 1 << 19),
    )(arrived)


def write_kernel(numbers, arrived, cache, new_cache):
    t = numbers[4]
    rows = jnp.concatenate([arrived[Y_ORDER.index(row), :16].astype(jnp.float32) for row in range(NY)], axis=0)
    rows = rows.astype(jnp.bfloat16)
    for conv in range(CONV):
        history, length = numbers[conv], numbers[2 + conv]
        within = (t - history) & (SEQ - 1)
        first = lax.div(history + within, SEQ)
        row = lax.broadcasted_iota(jnp.int32, (LOCAL, HEAD), 0) - first
        column = lax.broadcasted_iota(jnp.int32, (LOCAL, HEAD), 1)
        slot = (column & 3) * NY + (column >> 4)
        live = (((column >> 2) & 1) == conv) & (slot * SEQ + within < length) & (row == slot)
        written = (row >= 0) & (row < 32) & (row * SEQ + within < length)
        for half in range(2):
            place = jnp.where(live & (((column >> 3) & 1) == half), 1.0, 0.0).astype(jnp.bfloat16)
            placed = jnp.dot(place, rows, preferred_element_type=jnp.float32)
            lanes = slice(half * HEAD, half * HEAD + HEAD)
            kept = jnp.where(written, placed, cache[conv, :, lanes].astype(jnp.float32))
            new_cache[conv, :, lanes] = kept.astype(jnp.bfloat16)


def write(numbers, arrived, cache):
    return pl.pallas_call(
        write_kernel,
        in_specs=[SMEM] + [VMEM] * 2,
        out_specs=VMEM,
        out_shape=jax.ShapeDtypeStruct((CONV, LOCAL, FEATURE), jnp.bfloat16),
        **params(4 * CONV * LOCAL * HEAD * FEATURE, 1 << 20),
    )(numbers, arrived, cache)


def on_device(new_hidden, kv_weight, kv_cache, step_kv, queries, hist_len, new_len):
    x, y, core, z = (lax.axis_index(name) for name in ALL)
    t = (x * NY + y) * NC + core
    own = x * NC + core

    weight = exchange(split_weight(kv_weight), ("x", "y", "core"), SEQ_ORDER).reshape(WIDTH, FEATURE)

    swap = [(0, 1), (1, 0)]
    there, back = [], []
    for chip in range(NX):
        for side, step in ((0, NX - 1), (1, 1)):
            there.append((chip * NC + side, (chip + step) % NX * NC + side))
            back.append((chip * NC + side, (chip - step) % NX * NC + side))
    hidden = new_hidden.reshape(CONV * TURN_DEV, WIDTH)
    after = lax.ppermute(hidden, ("x", "core"), there)
    hidden, after = lax.optimization_barrier((hidden, after))
    before = lax.ppermute(hidden, ("x", "core"), back)
    near = jnp.concatenate([hidden, after], axis=0)
    far = jnp.concatenate([before, lax.ppermute(after, ("x", "core"), there)], axis=0)
    near_other = lax.ppermute(near, "core", swap)
    near_other, hist_len, new_len = lax.optimization_barrier((near_other, hist_len, new_len))
    numbers = jnp.concatenate([hist_len, new_len, jnp.stack([t, y, own, z])]).astype(jnp.int32)
    asked = queries.transpose(0, 2, 1, 3).reshape(CONV, QROWS, HEAD)
    steps = jnp.pad(step_kv.reshape(CONV, STEPS, FEATURE), ((0, 0), (0, 16 - STEPS), (0, 0)))
    cache = kv_cache.reshape(CONV, LOCAL, FEATURE)
    history_part = attend_history(numbers, cache, steps, asked)
    far, history_part = lax.optimization_barrier((far, history_part))
    blocks = [near, near_other, far, lax.ppermute(far, "core", swap)]

    def axis(size, place):
        shape = [1, 1, 1, 1]
        shape[place] = size
        return jnp.arange(size, dtype=jnp.int32).reshape(shape)

    history = hist_len.reshape(1, 1, CONV, 1)
    source_x = axis(NX, 3)

    def within_of(device):
        owner = device // NC * (NY * NC) + axis(NY, 1) * NC + device % NC
        return (owner - history) % SEQ

    within = within_of(axis(GROUP, 0))
    crossed = within // TURN_DEV ^ core
    place = jnp.where(within // TURN_DEV == 0, source_x - x, x - source_x) % NX
    place = jnp.where(place < 2, place, 7 - place) + crossed * 2
    column = place * SLICE + axis(CONV, 2) * TURN_DEV + within % TURN_DEV
    order = (column.reshape(ROWS, 1) == jnp.arange(ROWS, dtype=jnp.int32)[None, :]).astype(jnp.bfloat16)

    position = history + (source_x * NY + y) * SEQ + within_of(own)
    frequency = rope_base ** (-2.0 * jnp.arange(HEAD // 2, dtype=jnp.float32) / HEAD)
    angles = position.reshape(SLICE, 1).astype(jnp.float32) * frequency[None, :]
    cosine, sine = jnp.cos(angles), jnp.sin(angles)
    cosine = jnp.concatenate([cosine, cosine], axis=1)
    sine = jnp.concatenate([-sine, sine], axis=1)

    order, cosine, sine, asked = lax.optimization_barrier((order, cosine, sine, asked))
    partial = exchange(project(numbers, blocks, weight, order), ("kv", "x", "core"), SUM_ORDER)
    rows = exchange(attend(numbers, partial, cosine, sine, asked, history_part), ("y",), Y_ORDER)
    packed = exchange(combine(merge_kernel, (GROUP, PACK, HEAD), rows), ("x", "core"), GROUP_ORDER)
    new_cache = write(numbers, rows, cache)
    attended = combine(finish_kernel, (ALL_Q, HEAD), packed)
    attended = attended.reshape(CONV, QPK, STEPS, HEAD).transpose(0, 2, 1, 3)
    return attended, new_cache.reshape(kv_cache.shape)


def solution(mesh):
    split = Mesh(mesh.devices.reshape(NX, NY, NC, NZ), ALL)
    seq = ALL[:3]
    return jax.shard_map(
        on_device,
        mesh=split,
        in_specs=(
            P(None, seq, "kv"),
            P(("kv",) + seq, None),
            P(None, seq, "kv", None),
            P(None, None, "kv", None),
            P(None, None, "kv", None),
            P(),
            P(),
        ),
        out_specs=(P(None, None, "kv", None), P(None, seq, "kv", None)),
        check_vma=False,
    )
```

```python
import jax
import jax.numpy as jnp
from jax import lax
from jax.experimental import pallas as pl
from jax.experimental.pallas import tpu as pltpu
from jax.sharding import Mesh
from jax.sharding import PartitionSpec as P

rope_base = 1000000.0
NX, NY, NC, NZ = 4, 8, 2, 8
SEQ = NX * NY * NC
GROUP = NX * NC
ALL = ("x", "y", "core", "kv")
CONV, TURN_DEV, WIDTH, HEAD, FEATURE = 2, 32, 1536, 128, 256
ROWS, SLICE = 512, 64
LOCAL = 256
STEPS, QPK = 4, 12
QROWS = STEPS * QPK
ALL_Q = CONV * QROWS
PACK = ALL_Q + 16
PIECE = 32
SEQ_ORDER = [(2 * NY + 6 + 11 * place) % (NX * NY) * NC + core for place in range(NX * NY) for core in range(NC)]
SUM_ORDER = [(6 * GROUP + 2 * NC + 11 * place) % (NZ * GROUP) for place in range(NZ * GROUP)]
Y_ORDER = [(4 + place) % NY for place in range(NY)]
GROUP_ORDER = [(2 * NC + place) % GROUP for place in range(GROUP)]
VMEM_LIMIT = 48 * 1024 * 1024
SMEM = pl.BlockSpec(memory_space=pltpu.SMEM)
VMEM = pl.BlockSpec(memory_space=pltpu.VMEM)


def params(flops, nbytes):
    return dict(
        compiler_params=pltpu.CompilerParams(vmem_limit_bytes=VMEM_LIMIT),
        cost_estimate=pl.CostEstimate(flops=flops, bytes_accessed=nbytes, transcendentals=0),
    )


def exchange(value, names, order):
    return lax.all_to_all(value, names, split_axis=0, concat_axis=0, tiled=True, axis_index_groups=[order])


def lane_group(rows):
    return lax.broadcasted_iota(jnp.int32, (rows, HEAD), 1) // PIECE


def split_weight_kernel(source, out, weight):
    pltpu.sync_copy(source, weight)
    depth = weight.shape[0]
    group = lane_group(depth)
    for c in range(GROUP):
        tiles = []
        for half in range(2):
            tile = jnp.zeros((depth, HEAD), jnp.float32)
            for head in range(4 * half, 4 * half + 4):
                start = head * FEATURE + c // 4 * HEAD
                columns = weight[:, start : start + HEAD].astype(jnp.float32)
                tile = jnp.where(group == (c + head) % 4, columns, tile)
            tiles.append(tile)
        columns = jnp.concatenate(tiles, axis=1).astype(jnp.bfloat16)
        for y in range(NY):
            out[SEQ_ORDER.index(c // NC * (NY * NC) + y * NC + c % NC)] = columns


def split_weight(weight):
    depth = weight.shape[0]
    return pl.pallas_call(
        split_weight_kernel,
        in_specs=[pl.BlockSpec(memory_space=pltpu.HBM)],
        scratch_shapes=[pltpu.VMEM(weight.shape, weight.dtype)],
        out_shape=jax.ShapeDtypeStruct((SEQ, depth, FEATURE), jnp.bfloat16),
        **params(1 << 20, 1 << 20),
    )(weight)


def project_kernel(numbers, near, near_other, far, far_other, weight, order, out):
    rows = jnp.concatenate([near[...], near_other[...], far[...], far_other[...]], axis=0)
    run = WIDTH // (NX * NY)
    starts = [SEQ_ORDER.index(chip * NC) // NC * run for chip in range(NX * NY)]
    weights = jnp.concatenate([weight[start : start + run] for start in starts], axis=0)
    partial = jnp.dot(rows, weights, preferred_element_type=jnp.float32).astype(jnp.bfloat16)
    half_rows = ROWS // 2
    halves = [
        jnp.dot(order[start : start + half_rows], partial, preferred_element_type=jnp.float32)
        for start in (0, half_rows)
    ]
    own = numbers[6]
    group = lane_group(16)
    for owner in range(GROUP):
        for half in range(2):
            turned = []
            for part in range(4):
                start = owner % (GROUP // 2) * SLICE + part * 16
                tile = halves[owner // (GROUP // 2)][start : start + 16, half * HEAD : half * HEAD + HEAD]
                turned.append(pltpu.roll(tile, part * PIECE, 1) if part else tile)
            for head in range(4 * half, 4 * half + 4):
                message = turned[0]
                for part in range(1, 4):
                    message = jnp.where(group == ((own + head + part) & 3), turned[part], message)
                out[SUM_ORDER.index(head * GROUP + owner)] = message.astype(jnp.bfloat16)


def project(numbers, blocks, weight, order):
    return pl.pallas_call(
        project_kernel,
        in_specs=[SMEM] + [VMEM] * 6,
        out_specs=VMEM,
        out_shape=jax.ShapeDtypeStruct((NZ * GROUP, 16, HEAD), jnp.bfloat16),
        **params(2 * ROWS * WIDTH * FEATURE, 3 << 20),
    )(numbers, *blocks, weight, order)


def pack(average, row):
    high = row.astype(jnp.bfloat16).astype(jnp.float32)
    middle = (row - high).astype(jnp.bfloat16).astype(jnp.float32)
    low = row - high - middle
    place = lax.broadcasted_iota(jnp.int32, (16, HEAD), 0)
    stats = jnp.where(place == 0, high, jnp.where(place == 1, middle, jnp.where(place == 2, low, 0.0)))
    return jnp.concatenate([average, stats], axis=0).astype(jnp.bfloat16)


def diagonal(first):
    row = lax.broadcasted_iota(jnp.int32, (ALL_Q, HEAD), 0)
    return row + first == lax.broadcasted_iota(jnp.int32, (ALL_Q, HEAD), 1)


def merge(parts, first):
    rows = []
    for part in parts:
        stats = part[first + ALL_Q : first + PACK].astype(jnp.float32)
        rows.append(stats[0:1] + stats[1:2] + stats[2:3])
    lses = jnp.concatenate(rows, axis=0)
    top = jnp.max(lses, axis=0, keepdims=True)
    weights = jnp.exp(lses - top)
    total = jnp.sum(weights, axis=0, keepdims=True)
    weights = weights / total
    on_diagonal = diagonal(first)
    summed = jnp.zeros((ALL_Q, HEAD), jnp.float32)
    spread = [
        jnp.where(on_diagonal, weights[index : index + 1], 0.0).astype(jnp.bfloat16)
        for index in range(len(parts))
    ]
    for index in range(0, len(parts), 2):
        pair = jnp.concatenate(spread[index : index + 2], axis=1)
        both = jnp.concatenate(parts[index : index + 2], axis=0)
        summed += jnp.dot(pair, both, preferred_element_type=jnp.float32)
    return summed, top + jnp.log(total)


def history_kernel(numbers, cache, step_kv, queries, summed, tops, totals):
    t = numbers[4]
    for conv in range(CONV):
        history, length = numbers[conv], numbers[2 + conv]
        query = queries[conv]
        keys = [cache[conv, :, :HEAD], step_kv[conv, :, :HEAD]]
        values = [cache[conv, :, HEAD:], step_kv[conv, :, HEAD:]]
        position = lax.broadcasted_iota(jnp.int32, (QROWS, LOCAL), 1) * SEQ + t
        step = lax.broadcasted_iota(jnp.int32, (QROWS, 16), 1)
        asked = lax.broadcasted_iota(jnp.int32, (QROWS, 16), 0) & 3
        visible = [
            position < history,
            (step <= asked) & (((history + length + step) & (SEQ - 1)) == t),
        ]
        scores = [score(query, rows) for rows in keys]
        top = jnp.maximum(*[largest(one, seen) for one, seen in zip(scores, visible)])
        weights = [jnp.where(seen, jnp.exp(one - top), 0.0) for one, seen in zip(scores, visible)]
        total = sum(jnp.sum(weight, axis=1, keepdims=True) for weight in weights)
        rows = slice(conv * QROWS, conv * QROWS + QROWS)
        summed[rows] = sum(blend(weight, value) for weight, value in zip(weights, values))
        tops[rows] = jnp.broadcast_to(top, (QROWS, HEAD))
        totals[rows] = jnp.broadcast_to(total, (QROWS, HEAD))


def score(query, rows):
    contract = (((1,), (1,)), ((), ()))
    return lax.dot_general(query, rows, contract, preferred_element_type=jnp.float32) * HEAD ** (-0.5)


def largest(scores, seen):
    return jnp.max(jnp.where(seen, scores, -3e38), axis=1, keepdims=True)


def blend(weights, rows):
    return jnp.dot(weights.astype(jnp.bfloat16), rows, preferred_element_type=jnp.float32)


def attend_history(numbers, cache, step_kv, queries):
    return pl.pallas_call(
        history_kernel,
        in_specs=[SMEM] + [VMEM] * 3,
        out_specs=[VMEM] * 3,
        out_shape=[jax.ShapeDtypeStruct((ALL_Q, HEAD), jnp.float32)] * 3,
        **params(2 * ALL_Q * LOCAL * FEATURE, 1 << 20),
    )(numbers, cache, step_kv, queries)


def attend_kernel(numbers, arrived, cosine, sine, queries, summed, tops, totals, out):
    y, own, z = numbers[5], numbers[6], numbers[7]
    group = lane_group(16)
    sums = []
    for c in range(GROUP):
        total = arrived[SUM_ORDER.index(c)].astype(jnp.float32)
        for plane in range(1, NZ):
            total += arrived[SUM_ORDER.index(plane * GROUP + c)].astype(jnp.float32)
        sums.append(total)
    halves = []
    for tile in range(2):
        pieces = []
        for part in range(4):
            piece = sums[4 * tile]
            for c in range(4 * tile + 1, 4 * tile + 4):
                piece = jnp.where(group == ((c + z + part) & 3), sums[c], piece)
            pieces.append(pltpu.roll(piece, HEAD - part * PIECE, 1) if part else piece)
        halves.append(jnp.concatenate(pieces, axis=0))
    key, value = halves
    key = key * cosine[...] + pltpu.roll(key, HEAD // 2, 1) * sine[...]
    for row in range(NY):
        both = jnp.concatenate([key[row * 8 : row * 8 + 8], value[row * 8 : row * 8 + 8]], axis=0)
        out[Y_ORDER.index(row), :16] = both.astype(jnp.bfloat16)
    key, value = key.astype(jnp.bfloat16), value.astype(jnp.bfloat16)

    asker = lax.broadcasted_iota(jnp.int32, (ALL_Q, SLICE), 0) >= QROWS
    row = lax.broadcasted_iota(jnp.int32, (ALL_Q, SLICE), 1)
    history = jnp.where(asker, numbers[1], numbers[0])
    length = jnp.where(asker, numbers[3], numbers[2])
    owner = own // NC * (NY * NC) + (row >> 3) * NC + own % NC
    offset = ((row & 3) * NY + y) * SEQ + ((owner - history) & (SEQ - 1))
    visible = (((row >> 2) & 1) == asker.astype(jnp.int32)) & (offset < length)
    scores = score(jnp.concatenate([queries[0], queries[1]], axis=0), key)
    old_top = tops[:, :1]
    top = jnp.maximum(old_top, largest(scores, visible))
    weights = jnp.where(visible, jnp.exp(scores - top), 0.0)
    kept = jnp.exp(old_top - top)
    total = totals[:, :1] * kept + jnp.sum(weights, axis=1, keepdims=True)
    average = (summed[...] * kept + blend(weights, value)) / total
    lse = jnp.sum(jnp.where(diagonal(16), top + jnp.log(total), 0.0), axis=0, keepdims=True)
    packed = pack(average, lse)
    for row in range(NY):
        out[row, 16:] = packed


def attend(numbers, arrived, cosine, sine, queries, history):
    return pl.pallas_call(
        attend_kernel,
        in_specs=[SMEM] + [VMEM] * 7,
        out_specs=VMEM,
        out_shape=jax.ShapeDtypeStruct((NY, 16 + PACK, HEAD), jnp.bfloat16),
        **params(4 * ALL_Q * SLICE * HEAD, 1 << 20),
    )(numbers, arrived, cosine, sine, queries, *history)


def merge_kernel(arrived, out):
    average, lse = merge([arrived[row] for row in range(NY)], 16)
    lse = pltpu.roll(jnp.broadcast_to(lse, (8, HEAD)), HEAD - 16, 1)[0:1]
    packed = pack(average, lse)
    for device in range(GROUP):
        out[device] = packed


def finish_kernel(arrived, out):
    rest = jnp.zeros((HEAD - PACK, HEAD), jnp.bfloat16)
    parts = [jnp.concatenate([arrived[device], rest], axis=0) for device in range(GROUP)]
    out[...] = merge(parts, 0)[0].astype(jnp.bfloat16)


def combine(kernel, shape, arrived):
    return pl.pallas_call(
        kernel,
        out_shape=jax.ShapeDtypeStruct(shape, jnp.bfloat16),
        **params(PACK * HEAD * 32, 1 << 19),
    )(arrived)


def write_kernel(numbers, arrived, cache, new_cache):
    t = numbers[4]
    rows = jnp.concatenate([arrived[Y_ORDER.index(row), :16].astype(jnp.float32) for row in range(NY)], axis=0)
    rows = rows.astype(jnp.bfloat16)
    for conv in range(CONV):
        history, length = numbers[conv], numbers[2 + conv]
        within = (t - history) & (SEQ - 1)
        first = lax.div(history + within, SEQ)
        row = lax.broadcasted_iota(jnp.int32, (LOCAL, HEAD), 0) - first
        column = lax.broadcasted_iota(jnp.int32, (LOCAL, HEAD), 1)
        slot = (column & 3) * NY + (column >> 4)
        live = (((column >> 2) & 1) == conv) & (slot * SEQ + within < length) & (row == slot)
        written = (row >= 0) & (row < 32) & (row * SEQ + within < length)
        for half in range(2):
            place = jnp.where(live & (((column >> 3) & 1) == half), 1.0, 0.0).astype(jnp.bfloat16)
            placed = jnp.dot(place, rows, preferred_element_type=jnp.float32)
            lanes = slice(half * HEAD, half * HEAD + HEAD)
            kept = jnp.where(written, placed, cache[conv, :, lanes].astype(jnp.float32))
            new_cache[conv, :, lanes] = kept.astype(jnp.bfloat16)


def write(numbers, arrived, cache):
    return pl.pallas_call(
        write_kernel,
        in_specs=[SMEM] + [VMEM] * 2,
        out_specs=VMEM,
        out_shape=jax.ShapeDtypeStruct((CONV, LOCAL, FEATURE), jnp.bfloat16),
        **params(4 * CONV * LOCAL * HEAD * FEATURE, 1 << 20),
    )(numbers, arrived, cache)


def on_device(new_hidden, kv_weight, kv_cache, step_kv, queries, hist_len, new_len):
    x, y, core, z = (lax.axis_index(name) for name in ALL)
    t = (x * NY + y) * NC + core
    own = x * NC + core

    weight = exchange(split_weight(kv_weight), ("x", "y", "core"), SEQ_ORDER).reshape(WIDTH, FEATURE)

    swap = [(0, 1), (1, 0)]
    there, back = [], []
    for chip in range(NX):
        for side, step in ((0, NX - 1), (1, 1)):
            there.append((chip * NC + side, (chip + step) % NX * NC + side))
            back.append((chip * NC + side, (chip - step) % NX * NC + side))
    hidden = new_hidden.reshape(CONV * TURN_DEV, WIDTH)
    after = lax.ppermute(hidden, ("x", "core"), there)
    hidden, after = lax.optimization_barrier((hidden, after))
    before = lax.ppermute(hidden, ("x", "core"), back)
    near = jnp.concatenate([hidden, after], axis=0)
    far = jnp.concatenate([before, lax.ppermute(after, ("x", "core"), there)], axis=0)
    near_other = lax.ppermute(near, "core", swap)
    near_other, hist_len, new_len = lax.optimization_barrier((near_other, hist_len, new_len))
    numbers = jnp.concatenate([hist_len, new_len, jnp.stack([t, y, own, z])]).astype(jnp.int32)
    asked = queries.transpose(0, 2, 1, 3).reshape(CONV, QROWS, HEAD)
    steps = jnp.pad(step_kv.reshape(CONV, STEPS, FEATURE), ((0, 0), (0, 16 - STEPS), (0, 0)))
    cache = kv_cache.reshape(CONV, LOCAL, FEATURE)
    history_part = attend_history(numbers, cache, steps, asked)
    far, history_part = lax.optimization_barrier((far, history_part))
    blocks = [near, near_other, far, lax.ppermute(far, "core", swap)]

    def axis(size, place):
        shape = [1, 1, 1, 1]
        shape[place] = size
        return jnp.arange(size, dtype=jnp.int32).reshape(shape)

    history = hist_len.reshape(1, 1, CONV, 1)
    source_x = axis(NX, 3)

    def within_of(device):
        owner = device // NC * (NY * NC) + axis(NY, 1) * NC + device % NC
        return (owner - history) % SEQ

    within = within_of(axis(GROUP, 0))
    crossed = within // TURN_DEV ^ core
    place = jnp.where(within // TURN_DEV == 0, source_x - x, x - source_x) % NX
    place = jnp.where(place < 2, place, 7 - place) + crossed * 2
    column = place * SLICE + axis(CONV, 2) * TURN_DEV + within % TURN_DEV
    order = (column.reshape(ROWS, 1) == jnp.arange(ROWS, dtype=jnp.int32)[None, :]).astype(jnp.bfloat16)

    position = history + (source_x * NY + y) * SEQ + within_of(own)
    frequency = rope_base ** (-2.0 * jnp.arange(HEAD // 2, dtype=jnp.float32) / HEAD)
    angles = position.reshape(SLICE, 1).astype(jnp.float32) * frequency[None, :]
    cosine, sine = jnp.cos(angles), jnp.sin(angles)
    cosine = jnp.concatenate([cosine, cosine], axis=1)
    sine = jnp.concatenate([-sine, sine], axis=1)

    order, cosine, sine, asked = lax.optimization_barrier((order, cosine, sine, asked))
    partial = exchange(project(numbers, blocks, weight, order), ("kv", "x", "core"), SUM_ORDER)
    rows = exchange(attend(numbers, partial, cosine, sine, asked, history_part), ("y",), Y_ORDER)
    packed = exchange(combine(merge_kernel, (GROUP, PACK, HEAD), rows), ("x", "core"), GROUP_ORDER)
    new_cache = write(numbers, rows, cache)
    attended = combine(finish_kernel, (ALL_Q, HEAD), packed)
    attended = attended.reshape(CONV, QPK, STEPS, HEAD).transpose(0, 2, 1, 3)
    return attended, new_cache.reshape(kv_cache.shape)


def solution(mesh):
    split = Mesh(mesh.devices.reshape(NX, NY, NC, NZ), ALL)
    seq = ALL[:3]
    return jax.shard_map(
        on_device,
        mesh=split,
        in_specs=(
            P(None, seq, "kv"),
            P(("kv",) + seq, None),
            P(None, seq, "kv", None),
            P(None, None, "kv", None),
            P(None, None, "kv", None),
            P(),
            P(),
        ),
        out_specs=(P(None, None, "kv", None), P(None, seq, "kv", None)),
        check_vma=False,
    )
```

```python
import jax
import jax.numpy as jnp
from jax import lax
from jax.experimental import pallas as pl
from jax.experimental.pallas import tpu as pltpu
from jax.sharding import Mesh
from jax.sharding import PartitionSpec as P

rope_base = 1000000.0
NX, NY, NC, NZ = 4, 8, 2, 8
SEQ = NX * NY * NC
GROUP = NX * NC
ALL = ("x", "y", "core", "kv")
CONV, TURN_DEV, WIDTH, HEAD, FEATURE = 2, 32, 1536, 128, 256
ROWS, SLICE = 512, 64
LOCAL = 256
STEPS, QPK = 4, 12
QROWS = STEPS * QPK
ALL_Q = CONV * QROWS
PACK = ALL_Q + 16
PIECE = 32
SEQ_ORDER = [((2 * NY + 6) * NC + place) % SEQ for place in range(SEQ)]
SUM_ORDER = [(6 * GROUP + 2 * NC + 11 * place) % (NZ * GROUP) for place in range(NZ * GROUP)]
Y_ORDER = [(4 + place) % NY for place in range(NY)]
GROUP_ORDER = [(2 * NC + place) % GROUP for place in range(GROUP)]
VMEM_LIMIT = 48 * 1024 * 1024
SMEM = pl.BlockSpec(memory_space=pltpu.SMEM)
VMEM = pl.BlockSpec(memory_space=pltpu.VMEM)


def params(flops, nbytes):
    return dict(
        compiler_params=pltpu.CompilerParams(vmem_limit_bytes=VMEM_LIMIT),
        cost_estimate=pl.CostEstimate(flops=flops, bytes_accessed=nbytes, transcendentals=0),
    )


def exchange(value, names, order):
    return lax.all_to_all(value, names, split_axis=0, concat_axis=0, tiled=True, axis_index_groups=[order])


def lane_group(rows):
    return lax.broadcasted_iota(jnp.int32, (rows, HEAD), 1) // PIECE


def split_weight_kernel(source, out, weight):
    pltpu.sync_copy(source, weight)
    depth = weight.shape[0]
    group = lane_group(depth)
    for c in range(GROUP):
        tiles = []
        for half in range(2):
            tile = jnp.zeros((depth, HEAD), jnp.float32)
            for head in range(4 * half, 4 * half + 4):
                start = head * FEATURE + c // 4 * HEAD
                columns = weight[:, start : start + HEAD].astype(jnp.float32)
                tile = jnp.where(group == (c + head) % 4, columns, tile)
            tiles.append(tile)
        columns = jnp.concatenate(tiles, axis=1).astype(jnp.bfloat16)
        for y in range(NY):
            out[SEQ_ORDER.index(c // NC * (NY * NC) + y * NC + c % NC)] = columns


def split_weight(weight):
    depth = weight.shape[0]
    return pl.pallas_call(
        split_weight_kernel,
        in_specs=[pl.BlockSpec(memory_space=pltpu.HBM)],
        scratch_shapes=[pltpu.VMEM(weight.shape, weight.dtype)],
        out_shape=jax.ShapeDtypeStruct((SEQ, depth, FEATURE), jnp.bfloat16),
        **params(1 << 20, 1 << 20),
    )(weight)


def project_kernel(numbers, near, near_other, far, far_other, weight, order, out):
    rows = jnp.concatenate([near[...], near_other[...], far[...], far_other[...]], axis=0)
    run = WIDTH // (NX * NY)
    starts = [SEQ_ORDER.index(chip * NC) // NC * run for chip in range(NX * NY)]
    weights = jnp.concatenate([weight[start : start + run] for start in starts], axis=0)
    partial = jnp.dot(rows, weights, preferred_element_type=jnp.float32).astype(jnp.bfloat16)
    half_rows = ROWS // 2
    halves = [
        jnp.dot(order[start : start + half_rows], partial, preferred_element_type=jnp.float32)
        for start in (0, half_rows)
    ]
    own = numbers[6]
    group = lane_group(16)
    for owner in range(GROUP):
        for half in range(2):
            turned = []
            for part in range(4):
                start = owner % (GROUP // 2) * SLICE + part * 16
                tile = halves[owner // (GROUP // 2)][start : start + 16, half * HEAD : half * HEAD + HEAD]
                turned.append(pltpu.roll(tile, part * PIECE, 1) if part else tile)
            for head in range(4 * half, 4 * half + 4):
                message = turned[0]
                for part in range(1, 4):
                    message = jnp.where(group == ((own + head + part) & 3), turned[part], message)
                out[SUM_ORDER.index(head * GROUP + owner)] = message.astype(jnp.bfloat16)


def project(numbers, blocks, weight, order):
    return pl.pallas_call(
        project_kernel,
        in_specs=[SMEM] + [VMEM] * 6,
        out_specs=VMEM,
        out_shape=jax.ShapeDtypeStruct((NZ * GROUP, 16, HEAD), jnp.bfloat16),
        **params(2 * ROWS * WIDTH * FEATURE, 3 << 20),
    )(numbers, *blocks, weight, order)


def pack(average, row):
    high = row.astype(jnp.bfloat16).astype(jnp.float32)
    middle = (row - high).astype(jnp.bfloat16).astype(jnp.float32)
    low = row - high - middle
    place = lax.broadcasted_iota(jnp.int32, (16, HEAD), 0)
    stats = jnp.where(place == 0, high, jnp.where(place == 1, middle, jnp.where(place == 2, low, 0.0)))
    return jnp.concatenate([average, stats], axis=0).astype(jnp.bfloat16)


def diagonal(first):
    row = lax.broadcasted_iota(jnp.int32, (ALL_Q, HEAD), 0)
    return row + first == lax.broadcasted_iota(jnp.int32, (ALL_Q, HEAD), 1)


def merge(parts, first):
    rows = []
    for part in parts:
        stats = part[first + ALL_Q : first + PACK].astype(jnp.float32)
        rows.append(stats[0:1] + stats[1:2] + stats[2:3])
    lses = jnp.concatenate(rows, axis=0)
    top = jnp.max(lses, axis=0, keepdims=True)
    weights = jnp.exp(lses - top)
    total = jnp.sum(weights, axis=0, keepdims=True)
    weights = weights / total
    on_diagonal = diagonal(first)
    summed = jnp.zeros((ALL_Q, HEAD), jnp.float32)
    spread = [
        jnp.where(on_diagonal, weights[index : index + 1], 0.0).astype(jnp.bfloat16)
        for index in range(len(parts))
    ]
    for index in range(0, len(parts), 2):
        pair = jnp.concatenate(spread[index : index + 2], axis=1)
        both = jnp.concatenate(parts[index : index + 2], axis=0)
        summed += jnp.dot(pair, both, preferred_element_type=jnp.float32)
    return summed, top + jnp.log(total)


def history_kernel(numbers, cache, step_kv, queries, summed, tops, totals):
    t = numbers[4]
    for conv in range(CONV):
        history, length = numbers[conv], numbers[2 + conv]
        query = queries[conv]
        keys = [cache[conv, :, :HEAD], step_kv[conv, :, :HEAD]]
        values = [cache[conv, :, HEAD:], step_kv[conv, :, HEAD:]]
        position = lax.broadcasted_iota(jnp.int32, (QROWS, LOCAL), 1) * SEQ + t
        step = lax.broadcasted_iota(jnp.int32, (QROWS, 16), 1)
        asked = lax.broadcasted_iota(jnp.int32, (QROWS, 16), 0) & 3
        visible = [
            position < history,
            (step <= asked) & (((history + length + step) & (SEQ - 1)) == t),
        ]
        scores = [score(query, rows) for rows in keys]
        top = jnp.maximum(*[largest(one, seen) for one, seen in zip(scores, visible)])
        weights = [jnp.where(seen, jnp.exp(one - top), 0.0) for one, seen in zip(scores, visible)]
        total = sum(jnp.sum(weight, axis=1, keepdims=True) for weight in weights)
        rows = slice(conv * QROWS, conv * QROWS + QROWS)
        summed[rows] = sum(blend(weight, value) for weight, value in zip(weights, values))
        tops[rows] = jnp.broadcast_to(top, (QROWS, HEAD))
        totals[rows] = jnp.broadcast_to(total, (QROWS, HEAD))


def score(query, rows):
    contract = (((1,), (1,)), ((), ()))
    return lax.dot_general(query, rows, contract, preferred_element_type=jnp.float32) * HEAD ** (-0.5)


def largest(scores, seen):
    return jnp.max(jnp.where(seen, scores, -3e38), axis=1, keepdims=True)


def blend(weights, rows):
    return jnp.dot(weights.astype(jnp.bfloat16), rows, preferred_element_type=jnp.float32)


def attend_history(numbers, cache, step_kv, queries):
    return pl.pallas_call(
        history_kernel,
        in_specs=[SMEM] + [VMEM] * 3,
        out_specs=[VMEM] * 3,
        out_shape=[jax.ShapeDtypeStruct((ALL_Q, HEAD), jnp.float32)] * 3,
        **params(2 * ALL_Q * LOCAL * FEATURE, 1 << 20),
    )(numbers, cache, step_kv, queries)


def attend_kernel(numbers, arrived, cosine, sine, queries, summed, tops, totals, out):
    y, own, z = numbers[5], numbers[6], numbers[7]
    group = lane_group(16)
    sums = []
    for c in range(GROUP):
        total = arrived[SUM_ORDER.index(c)].astype(jnp.float32)
        for plane in range(1, NZ):
            total += arrived[SUM_ORDER.index(plane * GROUP + c)].astype(jnp.float32)
        sums.append(total)
    halves = []
    for tile in range(2):
        pieces = []
        for part in range(4):
            piece = sums[4 * tile]
            for c in range(4 * tile + 1, 4 * tile + 4):
                piece = jnp.where(group == ((c + z + part) & 3), sums[c], piece)
            pieces.append(pltpu.roll(piece, HEAD - part * PIECE, 1) if part else piece)
        halves.append(jnp.concatenate(pieces, axis=0))
    key, value = halves
    key = key * cosine[...] + pltpu.roll(key, HEAD // 2, 1) * sine[...]
    for row in range(NY):
        both = jnp.concatenate([key[row * 8 : row * 8 + 8], value[row * 8 : row * 8 + 8]], axis=0)
        out[Y_ORDER.index(row), :16] = both.astype(jnp.bfloat16)
    key, value = key.astype(jnp.bfloat16), value.astype(jnp.bfloat16)

    asker = lax.broadcasted_iota(jnp.int32, (ALL_Q, SLICE), 0) >= QROWS
    row = lax.broadcasted_iota(jnp.int32, (ALL_Q, SLICE), 1)
    history = jnp.where(asker, numbers[1], numbers[0])
    length = jnp.where(asker, numbers[3], numbers[2])
    owner = own // NC * (NY * NC) + (row >> 3) * NC + own % NC
    offset = ((row & 3) * NY + y) * SEQ + ((owner - history) & (SEQ - 1))
    visible = (((row >> 2) & 1) == asker.astype(jnp.int32)) & (offset < length)
    scores = score(jnp.concatenate([queries[0], queries[1]], axis=0), key)
    old_top = tops[:, :1]
    top = jnp.maximum(old_top, largest(scores, visible))
    weights = jnp.where(visible, jnp.exp(scores - top), 0.0)
    kept = jnp.exp(old_top - top)
    total = totals[:, :1] * kept + jnp.sum(weights, axis=1, keepdims=True)
    average = (summed[...] * kept + blend(weights, value)) / total
    lse = jnp.sum(jnp.where(diagonal(16), top + jnp.log(total), 0.0), axis=0, keepdims=True)
    packed = pack(average, lse)
    for row in range(NY):
        out[row, 16:] = packed


def attend(numbers, arrived, cosine, sine, queries, history):
    return pl.pallas_call(
        attend_kernel,
        in_specs=[SMEM] + [VMEM] * 7,
        out_specs=VMEM,
        out_shape=jax.ShapeDtypeStruct((NY, 16 + PACK, HEAD), jnp.bfloat16),
        **params(4 * ALL_Q * SLICE * HEAD, 1 << 20),
    )(numbers, arrived, cosine, sine, queries, *history)


def merge_kernel(arrived, out):
    average, lse = merge([arrived[row] for row in range(NY)], 16)
    lse = pltpu.roll(jnp.broadcast_to(lse, (8, HEAD)), HEAD - 16, 1)[0:1]
    packed = pack(average, lse)
    for device in range(GROUP):
        out[device] = packed


def finish_kernel(arrived, out):
    rest = jnp.zeros((HEAD - PACK, HEAD), jnp.bfloat16)
    parts = [jnp.concatenate([arrived[device], rest], axis=0) for device in range(GROUP)]
    out[...] = merge(parts, 0)[0].astype(jnp.bfloat16)


def combine(kernel, shape, arrived):
    return pl.pallas_call(
        kernel,
        out_shape=jax.ShapeDtypeStruct(shape, jnp.bfloat16),
        **params(PACK * HEAD * 32, 1 << 19),
    )(arrived)


def write_kernel(numbers, arrived, cache, new_cache):
    t = numbers[4]
    rows = jnp.concatenate([arrived[Y_ORDER.index(row), :16].astype(jnp.float32) for row in range(NY)], axis=0)
    rows = rows.astype(jnp.bfloat16)
    for conv in range(CONV):
        history, length = numbers[conv], numbers[2 + conv]
        within = (t - history) & (SEQ - 1)
        first = lax.div(history + within, SEQ)
        row = lax.broadcasted_iota(jnp.int32, (LOCAL, HEAD), 0) - first
        column = lax.broadcasted_iota(jnp.int32, (LOCAL, HEAD), 1)
        slot = (column & 3) * NY + (column >> 4)
        live = (((column >> 2) & 1) == conv) & (slot * SEQ + within < length) & (row == slot)
        written = (row >= 0) & (row < 32) & (row * SEQ + within < length)
        for half in range(2):
            place = jnp.where(live & (((column >> 3) & 1) == half), 1.0, 0.0).astype(jnp.bfloat16)
            placed = jnp.dot(place, rows, preferred_element_type=jnp.float32)
            lanes = slice(half * HEAD, half * HEAD + HEAD)
            kept = jnp.where(written, placed, cache[conv, :, lanes].astype(jnp.float32))
            new_cache[conv, :, lanes] = kept.astype(jnp.bfloat16)


def write(numbers, arrived, cache):
    return pl.pallas_call(
        write_kernel,
        in_specs=[SMEM] + [VMEM] * 2,
        out_specs=VMEM,
        out_shape=jax.ShapeDtypeStruct((CONV, LOCAL, FEATURE), jnp.bfloat16),
        **params(4 * CONV * LOCAL * HEAD * FEATURE, 1 << 20),
    )(numbers, arrived, cache)


def on_device(new_hidden, kv_weight, kv_cache, step_kv, queries, hist_len, new_len):
    x, y, core, z = (lax.axis_index(name) for name in ALL)
    t = (x * NY + y) * NC + core
    own = x * NC + core

    weight = exchange(split_weight(kv_weight), ("x", "y", "core"), SEQ_ORDER).reshape(WIDTH, FEATURE)

    swap = [(0, 1), (1, 0)]
    there, back = [], []
    for chip in range(NX):
        for side, step in ((0, NX - 1), (1, 1)):
            there.append((chip * NC + side, (chip + step) % NX * NC + side))
            back.append((chip * NC + side, (chip - step) % NX * NC + side))
    hidden = new_hidden.reshape(CONV * TURN_DEV, WIDTH)
    after = lax.ppermute(hidden, ("x", "core"), there)
    hidden, after = lax.optimization_barrier((hidden, after))
    before = lax.ppermute(hidden, ("x", "core"), back)
    near = jnp.concatenate([hidden, after], axis=0)
    far = jnp.concatenate([before, lax.ppermute(after, ("x", "core"), there)], axis=0)
    near_other = lax.ppermute(near, "core", swap)
    near_other, hist_len, new_len = lax.optimization_barrier((near_other, hist_len, new_len))
    numbers = jnp.concatenate([hist_len, new_len, jnp.stack([t, y, own, z])]).astype(jnp.int32)
    asked = queries.transpose(0, 2, 1, 3).reshape(CONV, QROWS, HEAD)
    steps = jnp.pad(step_kv.reshape(CONV, STEPS, FEATURE), ((0, 0), (0, 16 - STEPS), (0, 0)))
    cache = kv_cache.reshape(CONV, LOCAL, FEATURE)
    history_part = attend_history(numbers, cache, steps, asked)
    far, history_part = lax.optimization_barrier((far, history_part))
    blocks = [near, near_other, far, lax.ppermute(far, "core", swap)]

    def axis(size, place):
        shape = [1, 1, 1, 1]
        shape[place] = size
        return jnp.arange(size, dtype=jnp.int32).reshape(shape)

    history = hist_len.reshape(1, 1, CONV, 1)
    source_x = axis(NX, 3)

    def within_of(device):
        owner = device // NC * (NY * NC) + axis(NY, 1) * NC + device % NC
        return (owner - history) % SEQ

    within = within_of(axis(GROUP, 0))
    crossed = within // TURN_DEV ^ core
    place = jnp.where(within // TURN_DEV == 0, source_x - x, x - source_x) % NX
    place = jnp.where(place < 2, place, 7 - place) + crossed * 2
    column = place * SLICE + axis(CONV, 2) * TURN_DEV + within % TURN_DEV
    order = (column.reshape(ROWS, 1) == jnp.arange(ROWS, dtype=jnp.int32)[None, :]).astype(jnp.bfloat16)

    position = history + (source_x * NY + y) * SEQ + within_of(own)
    frequency = rope_base ** (-2.0 * jnp.arange(HEAD // 2, dtype=jnp.float32) / HEAD)
    angles = position.reshape(SLICE, 1).astype(jnp.float32) * frequency[None, :]
    cosine, sine = jnp.cos(angles), jnp.sin(angles)
    cosine = jnp.concatenate([cosine, cosine], axis=1)
    sine = jnp.concatenate([-sine, sine], axis=1)

    order, cosine, sine, asked = lax.optimization_barrier((order, cosine, sine, asked))
    partial = exchange(project(numbers, blocks, weight, order), ("kv", "x", "core"), SUM_ORDER)
    rows = exchange(attend(numbers, partial, cosine, sine, asked, history_part), ("y",), Y_ORDER)
    packed = exchange(combine(merge_kernel, (GROUP, PACK, HEAD), rows), ("x", "core"), GROUP_ORDER)
    new_cache = write(numbers, rows, cache)
    attended = combine(finish_kernel, (ALL_Q, HEAD), packed)
    attended = attended.reshape(CONV, QPK, STEPS, HEAD).transpose(0, 2, 1, 3)
    return attended, new_cache.reshape(kv_cache.shape)


def solution(mesh):
    split = Mesh(mesh.devices.reshape(NX, NY, NC, NZ), ALL)
    seq = ALL[:3]
    return jax.shard_map(
        on_device,
        mesh=split,
        in_specs=(
            P(None, seq, "kv"),
            P(("kv",) + seq, None),
            P(None, seq, "kv", None),
            P(None, None, "kv", None),
            P(None, None, "kv", None),
            P(),
            P(),
        ),
        out_specs=(P(None, None, "kv", None), P(None, seq, "kv", None)),
        check_vma=False,
    )
```

```python
import jax
import jax.numpy as jnp
from jax import lax
from jax.experimental import pallas as pl
from jax.experimental.pallas import tpu as pltpu
from jax.sharding import Mesh
from jax.sharding import PartitionSpec as P

rope_base = 1000000.0
NX, NY, NC, NZ = 4, 8, 2, 8
SEQ = NX * NY * NC
GROUP = NX * NC
ALL = ("x", "y", "core", "kv")
CONV, TURN_DEV, WIDTH, HEAD, FEATURE = 2, 32, 1536, 128, 256
ROWS, SLICE = 512, 64
LOCAL = 256
STEPS, QPK = 4, 12
QROWS = STEPS * QPK
ALL_Q = CONV * QROWS
PACK = ALL_Q + 16
PIECE = 32
FIRST_SEQ = (2 * NY + 6) * NC
FIRST = 5 * GROUP + 2 * NC
FIRST_Y = 4
FIRST_GROUP = 2 * NC
VMEM_LIMIT = 48 * 1024 * 1024
SMEM = pl.BlockSpec(memory_space=pltpu.SMEM)
VMEM = pl.BlockSpec(memory_space=pltpu.VMEM)


def params(flops, nbytes):
    return dict(
        compiler_params=pltpu.CompilerParams(vmem_limit_bytes=VMEM_LIMIT),
        cost_estimate=pl.CostEstimate(flops=flops, bytes_accessed=nbytes, transcendentals=0),
    )


def exchange(value, names, first=0):
    size = value.shape[0]
    groups = [[(place + first) % size for place in range(size)]] if first else None
    return lax.all_to_all(value, names, split_axis=0, concat_axis=0, tiled=True, axis_index_groups=groups)


def lane_group(rows):
    return lax.broadcasted_iota(jnp.int32, (rows, HEAD), 1) // PIECE


def split_weight_kernel(source, out, weight):
    pltpu.sync_copy(source, weight)
    depth = weight.shape[0]
    group = lane_group(depth)
    for c in range(GROUP):
        tiles = []
        for half in range(2):
            tile = jnp.zeros((depth, HEAD), jnp.float32)
            for head in range(4 * half, 4 * half + 4):
                start = head * FEATURE + c // 4 * HEAD
                columns = weight[:, start : start + HEAD].astype(jnp.float32)
                tile = jnp.where(group == (c + head) % 4, columns, tile)
            tiles.append(tile)
        columns = jnp.concatenate(tiles, axis=1).astype(jnp.bfloat16)
        for y in range(NY):
            out[(c // NC * (NY * NC) + y * NC + c % NC - FIRST_SEQ) % SEQ] = columns


def split_weight(weight):
    depth = weight.shape[0]
    return pl.pallas_call(
        split_weight_kernel,
        in_specs=[pl.BlockSpec(memory_space=pltpu.HBM)],
        scratch_shapes=[pltpu.VMEM(weight.shape, weight.dtype)],
        out_shape=jax.ShapeDtypeStruct((SEQ, depth, FEATURE), jnp.bfloat16),
        **params(1 << 20, 1 << 20),
    )(weight)


def project_kernel(numbers, near, near_other, far, far_other, weight, order, out):
    rows = jnp.concatenate([near[...], near_other[...], far[...], far_other[...]], axis=0)
    start = (SEQ - FIRST_SEQ) * (WIDTH // SEQ)
    weights = jnp.concatenate([weight[start:], weight[:start]], axis=0)
    partial = jnp.dot(rows, weights, preferred_element_type=jnp.float32).astype(jnp.bfloat16)
    half_rows = ROWS // 2
    halves = [
        jnp.dot(order[start : start + half_rows], partial, preferred_element_type=jnp.float32)
        for start in (0, half_rows)
    ]
    own = numbers[6]
    group = lane_group(16)
    for owner in range(GROUP):
        for half in range(2):
            turned = []
            for part in range(4):
                start = owner % (GROUP // 2) * SLICE + part * 16
                tile = halves[owner // (GROUP // 2)][start : start + 16, half * HEAD : half * HEAD + HEAD]
                turned.append(pltpu.roll(tile, part * PIECE, 1) if part else tile)
            for head in range(4 * half, 4 * half + 4):
                message = turned[0]
                for part in range(1, 4):
                    message = jnp.where(group == ((own + head + part) & 3), turned[part], message)
                out[(head * GROUP + owner - FIRST) % (NZ * GROUP)] = message.astype(jnp.bfloat16)


def project(numbers, blocks, weight, order):
    return pl.pallas_call(
        project_kernel,
        in_specs=[SMEM] + [VMEM] * 6,
        out_specs=VMEM,
        out_shape=jax.ShapeDtypeStruct((NZ * GROUP, 16, HEAD), jnp.bfloat16),
        **params(2 * ROWS * WIDTH * FEATURE, 3 << 20),
    )(numbers, *blocks, weight, order)


def pack(average, row):
    high = row.astype(jnp.bfloat16).astype(jnp.float32)
    middle = (row - high).astype(jnp.bfloat16).astype(jnp.float32)
    low = row - high - middle
    place = lax.broadcasted_iota(jnp.int32, (16, HEAD), 0)
    stats = jnp.where(place == 0, high, jnp.where(place == 1, middle, jnp.where(place == 2, low, 0.0)))
    return jnp.concatenate([average, stats], axis=0).astype(jnp.bfloat16)


def diagonal(first):
    row = lax.broadcasted_iota(jnp.int32, (ALL_Q, HEAD), 0)
    return row + first == lax.broadcasted_iota(jnp.int32, (ALL_Q, HEAD), 1)


def merge(parts, first):
    rows = []
    for part in parts:
        stats = part[first + ALL_Q : first + PACK].astype(jnp.float32)
        rows.append(stats[0:1] + stats[1:2] + stats[2:3])
    lses = jnp.concatenate(rows, axis=0)
    top = jnp.max(lses, axis=0, keepdims=True)
    weights = jnp.exp(lses - top)
    total = jnp.sum(weights, axis=0, keepdims=True)
    weights = weights / total
    on_diagonal = diagonal(first)
    summed = jnp.zeros((ALL_Q, HEAD), jnp.float32)
    spread = [
        jnp.where(on_diagonal, weights[index : index + 1], 0.0).astype(jnp.bfloat16)
        for index in range(len(parts))
    ]
    for index in range(0, len(parts), 2):
        pair = jnp.concatenate(spread[index : index + 2], axis=1)
        both = jnp.concatenate(parts[index : index + 2], axis=0)
        summed += jnp.dot(pair, both, preferred_element_type=jnp.float32)
    return summed, top + jnp.log(total)


def history_kernel(numbers, cache, step_kv, queries, summed, tops, totals):
    t = numbers[4]
    for conv in range(CONV):
        history, length = numbers[conv], numbers[2 + conv]
        query = queries[conv]
        keys = [cache[conv, :, :HEAD], step_kv[conv, :, :HEAD]]
        values = [cache[conv, :, HEAD:], step_kv[conv, :, HEAD:]]
        position = lax.broadcasted_iota(jnp.int32, (QROWS, LOCAL), 1) * SEQ + t
        step = lax.broadcasted_iota(jnp.int32, (QROWS, 16), 1)
        asked = lax.broadcasted_iota(jnp.int32, (QROWS, 16), 0) & 3
        visible = [
            position < history,
            (step <= asked) & (((history + length + step) & (SEQ - 1)) == t),
        ]
        scores = [score(query, rows) for rows in keys]
        top = jnp.maximum(*[largest(one, seen) for one, seen in zip(scores, visible)])
        weights = [jnp.where(seen, jnp.exp(one - top), 0.0) for one, seen in zip(scores, visible)]
        total = sum(jnp.sum(weight, axis=1, keepdims=True) for weight in weights)
        rows = slice(conv * QROWS, conv * QROWS + QROWS)
        summed[rows] = sum(blend(weight, value) for weight, value in zip(weights, values))
        tops[rows] = jnp.broadcast_to(top, (QROWS, HEAD))
        totals[rows] = jnp.broadcast_to(total, (QROWS, HEAD))


def score(query, rows):
    contract = (((1,), (1,)), ((), ()))
    return lax.dot_general(query, rows, contract, preferred_element_type=jnp.float32) * HEAD ** (-0.5)


def largest(scores, seen):
    return jnp.max(jnp.where(seen, scores, -3e38), axis=1, keepdims=True)


def blend(weights, rows):
    return jnp.dot(weights.astype(jnp.bfloat16), rows, preferred_element_type=jnp.float32)


def attend_history(numbers, cache, step_kv, queries):
    return pl.pallas_call(
        history_kernel,
        in_specs=[SMEM] + [VMEM] * 3,
        out_specs=[VMEM] * 3,
        out_shape=[jax.ShapeDtypeStruct((ALL_Q, HEAD), jnp.float32)] * 3,
        **params(2 * ALL_Q * LOCAL * FEATURE, 1 << 20),
    )(numbers, cache, step_kv, queries)


def attend_kernel(numbers, arrived, cosine, sine, queries, summed, tops, totals, out):
    y, own, z = numbers[5], numbers[6], numbers[7]
    group = lane_group(16)
    sums = []
    for c in range(GROUP):
        total = arrived[(c - FIRST) % (NZ * GROUP)].astype(jnp.float32)
        for plane in range(1, NZ):
            total += arrived[(plane * GROUP + c - FIRST) % (NZ * GROUP)].astype(jnp.float32)
        sums.append(total)
    halves = []
    for tile in range(2):
        pieces = []
        for part in range(4):
            piece = sums[4 * tile]
            for c in range(4 * tile + 1, 4 * tile + 4):
                piece = jnp.where(group == ((c + z + part) & 3), sums[c], piece)
            pieces.append(pltpu.roll(piece, HEAD - part * PIECE, 1) if part else piece)
        halves.append(jnp.concatenate(pieces, axis=0))
    key, value = halves
    key = key * cosine[...] + pltpu.roll(key, HEAD // 2, 1) * sine[...]
    for row in range(NY):
        both = jnp.concatenate([key[row * 8 : row * 8 + 8], value[row * 8 : row * 8 + 8]], axis=0)
        out[(row - FIRST_Y) % NY, :16] = both.astype(jnp.bfloat16)
    key, value = key.astype(jnp.bfloat16), value.astype(jnp.bfloat16)

    asker = lax.broadcasted_iota(jnp.int32, (ALL_Q, SLICE), 0) >= QROWS
    row = lax.broadcasted_iota(jnp.int32, (ALL_Q, SLICE), 1)
    history = jnp.where(asker, numbers[1], numbers[0])
    length = jnp.where(asker, numbers[3], numbers[2])
    owner = own // NC * (NY * NC) + (row >> 3) * NC + own % NC
    offset = ((row & 3) * NY + y) * SEQ + ((owner - history) & (SEQ - 1))
    visible = (((row >> 2) & 1) == asker.astype(jnp.int32)) & (offset < length)
    scores = score(jnp.concatenate([queries[0], queries[1]], axis=0), key)
    old_top = tops[:, :1]
    top = jnp.maximum(old_top, largest(scores, visible))
    weights = jnp.where(visible, jnp.exp(scores - top), 0.0)
    kept = jnp.exp(old_top - top)
    total = totals[:, :1] * kept + jnp.sum(weights, axis=1, keepdims=True)
    average = (summed[...] * kept + blend(weights, value)) / total
    lse = jnp.sum(jnp.where(diagonal(16), top + jnp.log(total), 0.0), axis=0, keepdims=True)
    packed = pack(average, lse)
    for row in range(NY):
        out[row, 16:] = packed


def attend(numbers, arrived, cosine, sine, queries, history):
    return pl.pallas_call(
        attend_kernel,
        in_specs=[SMEM] + [VMEM] * 7,
        out_specs=VMEM,
        out_shape=jax.ShapeDtypeStruct((NY, 16 + PACK, HEAD), jnp.bfloat16),
        **params(4 * ALL_Q * SLICE * HEAD, 1 << 20),
    )(numbers, arrived, cosine, sine, queries, *history)


def merge_kernel(arrived, out):
    average, lse = merge([arrived[row] for row in range(NY)], 16)
    lse = pltpu.roll(jnp.broadcast_to(lse, (8, HEAD)), HEAD - 16, 1)[0:1]
    packed = pack(average, lse)
    for device in range(GROUP):
        out[device] = packed


def finish_kernel(arrived, out):
    rest = jnp.zeros((HEAD - PACK, HEAD), jnp.bfloat16)
    parts = [jnp.concatenate([arrived[device], rest], axis=0) for device in range(GROUP)]
    out[...] = merge(parts, 0)[0].astype(jnp.bfloat16)


def combine(kernel, shape, arrived):
    return pl.pallas_call(
        kernel,
        out_shape=jax.ShapeDtypeStruct(shape, jnp.bfloat16),
        **params(PACK * HEAD * 32, 1 << 19),
    )(arrived)


def write_kernel(numbers, arrived, cache, new_cache):
    t = numbers[4]
    rows = jnp.concatenate([arrived[(row - FIRST_Y) % NY, :16].astype(jnp.float32) for row in range(NY)], axis=0)
    rows = rows.astype(jnp.bfloat16)
    for conv in range(CONV):
        history, length = numbers[conv], numbers[2 + conv]
        within = (t - history) & (SEQ - 1)
        first = lax.div(history + within, SEQ)
        row = lax.broadcasted_iota(jnp.int32, (LOCAL, HEAD), 0) - first
        column = lax.broadcasted_iota(jnp.int32, (LOCAL, HEAD), 1)
        slot = (column & 3) * NY + (column >> 4)
        live = (((column >> 2) & 1) == conv) & (slot * SEQ + within < length) & (row == slot)
        written = (row >= 0) & (row < 32) & (row * SEQ + within < length)
        for half in range(2):
            place = jnp.where(live & (((column >> 3) & 1) == half), 1.0, 0.0).astype(jnp.bfloat16)
            placed = jnp.dot(place, rows, preferred_element_type=jnp.float32)
            lanes = slice(half * HEAD, half * HEAD + HEAD)
            kept = jnp.where(written, placed, cache[conv, :, lanes].astype(jnp.float32))
            new_cache[conv, :, lanes] = kept.astype(jnp.bfloat16)


def write(numbers, arrived, cache):
    return pl.pallas_call(
        write_kernel,
        in_specs=[SMEM] + [VMEM] * 2,
        out_specs=VMEM,
        out_shape=jax.ShapeDtypeStruct((CONV, LOCAL, FEATURE), jnp.bfloat16),
        **params(4 * CONV * LOCAL * HEAD * FEATURE, 1 << 20),
    )(numbers, arrived, cache)


def on_device(new_hidden, kv_weight, kv_cache, step_kv, queries, hist_len, new_len):
    x, y, core, z = (lax.axis_index(name) for name in ALL)
    t = (x * NY + y) * NC + core
    own = x * NC + core

    weight = exchange(split_weight(kv_weight), ("x", "y", "core"), FIRST_SEQ).reshape(WIDTH, FEATURE)

    swap = [(0, 1), (1, 0)]
    there, back = [], []
    for chip in range(NX):
        for side, step in ((0, NX - 1), (1, 1)):
            there.append((chip * NC + side, (chip + step) % NX * NC + side))
            back.append((chip * NC + side, (chip - step) % NX * NC + side))
    hidden = new_hidden.reshape(CONV * TURN_DEV, WIDTH)
    after = lax.ppermute(hidden, ("x", "core"), there)
    hidden, after = lax.optimization_barrier((hidden, after))
    before = lax.ppermute(hidden, ("x", "core"), back)
    near = jnp.concatenate([hidden, after], axis=0)
    far = jnp.concatenate([before, lax.ppermute(after, ("x", "core"), there)], axis=0)
    near_other = lax.ppermute(near, "core", swap)
    near_other, hist_len, new_len = lax.optimization_barrier((near_other, hist_len, new_len))
    numbers = jnp.concatenate([hist_len, new_len, jnp.stack([t, y, own, z])]).astype(jnp.int32)
    asked = queries.transpose(0, 2, 1, 3).reshape(CONV, QROWS, HEAD)
    steps = jnp.pad(step_kv.reshape(CONV, STEPS, FEATURE), ((0, 0), (0, 16 - STEPS), (0, 0)))
    cache = kv_cache.reshape(CONV, LOCAL, FEATURE)
    history_part = attend_history(numbers, cache, steps, asked)
    far, history_part = lax.optimization_barrier((far, history_part))
    blocks = [near, near_other, far, lax.ppermute(far, "core", swap)]

    def axis(size, place):
        shape = [1, 1, 1, 1]
        shape[place] = size
        return jnp.arange(size, dtype=jnp.int32).reshape(shape)

    history = hist_len.reshape(1, 1, CONV, 1)
    source_x = axis(NX, 3)

    def within_of(device):
        owner = device // NC * (NY * NC) + axis(NY, 1) * NC + device % NC
        return (owner - history) % SEQ

    within = within_of(axis(GROUP, 0))
    crossed = within // TURN_DEV ^ core
    place = jnp.where(within // TURN_DEV == 0, source_x - x, x - source_x) % NX
    place = jnp.where(place < 2, place, 7 - place) + crossed * 2
    column = place * SLICE + axis(CONV, 2) * TURN_DEV + within % TURN_DEV
    order = (column.reshape(ROWS, 1) == jnp.arange(ROWS, dtype=jnp.int32)[None, :]).astype(jnp.bfloat16)

    position = history + (source_x * NY + y) * SEQ + within_of(own)
    frequency = rope_base ** (-2.0 * jnp.arange(HEAD // 2, dtype=jnp.float32) / HEAD)
    angles = position.reshape(SLICE, 1).astype(jnp.float32) * frequency[None, :]
    cosine, sine = jnp.cos(angles), jnp.sin(angles)
    cosine = jnp.concatenate([cosine, cosine], axis=1)
    sine = jnp.concatenate([-sine, sine], axis=1)

    order, cosine, sine, asked = lax.optimization_barrier((order, cosine, sine, asked))
    partial = exchange(project(numbers, blocks, weight, order), ("kv", "x", "core"), FIRST)
    rows = exchange(attend(numbers, partial, cosine, sine, asked, history_part), ("y",), FIRST_Y)
    packed = exchange(combine(merge_kernel, (GROUP, PACK, HEAD), rows), ("x", "core"), FIRST_GROUP)
    new_cache = write(numbers, rows, cache)
    attended = combine(finish_kernel, (ALL_Q, HEAD), packed)
    attended = attended.reshape(CONV, QPK, STEPS, HEAD).transpose(0, 2, 1, 3)
    return attended, new_cache.reshape(kv_cache.shape)


def solution(mesh):
    split = Mesh(mesh.devices.reshape(NX, NY, NC, NZ), ALL)
    seq = ALL[:3]
    return jax.shard_map(
        on_device,
        mesh=split,
        in_specs=(
            P(None, seq, "kv"),
            P(("kv",) + seq, None),
            P(None, seq, "kv", None),
            P(None, None, "kv", None),
            P(None, None, "kv", None),
            P(),
            P(),
        ),
        out_specs=(P(None, None, "kv", None), P(None, seq, "kv", None)),
        check_vma=False,
    )
```
